32 devices in a mesh: groups: 2 (over x), ctx: 16 (over z, y, core).
Axes of the slice: x: 2, y: 2, z: 4, core: 2. Of those that a mesh axis runs over, the one named last changes fastest.
Arguments:
- tokens: bfloat16 [4096, 2880], P(('groups', 'ctx')), parts along dimension 0, may hold values from -6 to 6
- lengths: int32 [8], P('groups'), parts along dimension 0, may hold values from 1 to 1536, 2048 in all
- attn_gain: float32 [2880], replicated, may hold values from 0.1 to 1.9
- w_query: bfloat16 [2880, 2048], P('ctx'), may hold values from -2 to 2
- w_key: bfloat16 [2880, 256], replicated, may hold values from -1 to 1
- w_value: bfloat16 [2880, 256], replicated, may hold values from -0.109375 to 0.109375
- sinks: float32 [32], replicated, may hold values from -2 to 4
- w_out: bfloat16 [2048, 2880], P('ctx'), may hold values from -0.5 to 0.5
- moe_gain: float32 [2880], replicated, may hold values from 0.1 to 1.9
- routes: int32 [4096, 4], P(('groups', 'ctx')), parts along dimension 0, may hold values from 0 to 7, all different within a row; in each aligned block of 128 rows (0 to 127, 128 to 255, ...) at most 68 rows name the same one
- route_weights: float32 [4096, 4], P(('groups', 'ctx')), parts along dimension 0, may hold values from 0.05 to 1
- w_gate: bfloat16 [16, 2880, 768], P('ctx'), may hold values from -0.109375 to 0.109375
- w_up: bfloat16 [16, 2880, 768], P('ctx'), may hold values from -0.109375 to 0.109375
- w_down: bfloat16 [16, 768, 2880], P('ctx'), may hold values from -0.15625 to 0.15625
Outputs:
- result: bfloat16 [4096, 2880], P(('groups', 'ctx')), parts along dimension 0
The draws below stay inside these ranges and needn't reach their ends.
There are 2 independent parts, one for each index of `groups`. The reference program is written for one: setup_inputs(seed, part) draws one part's arguments, and reference() takes and returns one part's arrays. A program takes and returns all parts, laid end to end along the dimension named above; an argument that names none is the same for every part. Nothing has to cross between parts.
Inputs may be any that keep to these rules, and one draw needn't show every extreme that they name: lengths of the 4 requests packed in order into the 2048 tokens; they sum to 2048. `routes`: each token names 4 different experts; among the 128 tokens of one index of ctx no expert is named by more than 68 tokens, a bound that some block reaches.
All inputs are finite; a program needn't handle non-finite values.
Results may differ from the reference program's by a relative error of at most 0.014.
Values may be sent and summed in bfloat16 or wider, within the bound.
No kernel may reach another device: no remote copies, remote signals or barrier semaphores. Data moves between devices by JAX's collectives and lax.ppermute only.
A program may use at most 128 MiB of HBM per device.

```python
import math
import jax
import jax.numpy as jnp
import numpy as np
from jax import lax

D = 2880
HEADS = 32
KV = 4
HD = 64
FF = 1536
SPLITS = 2
TOP = 4
DOCS = 4
TOK_DEV = 128
SEQ = 2048
SLABS = 16
EXPERTS = 8
FF_SLAB = 768
CAP = 68
N_CTX = 16


def key_matrix(base_key):
    source = jax.random.normal(jax.random.fold_in(base_key, 11), (D, KV * HD), jnp.float32)
    return jnp.clip(source, -4.0, 4.0) / math.sqrt(D)


def draw_w_key(key, part):
    return key_matrix(key).astype(jnp.bfloat16)


def draw_w_query(key, part):
    source = jax.random.normal(jax.random.fold_in(key, 12), (D, HEADS * HD), jnp.float32)
    query_mat = jnp.clip(source, -4.0, 4.0) / math.sqrt(D)
    return query_mat.astype(jnp.bfloat16)


def steps_of(own_key, extent, pieces, least, high):
    level = 1.0
    for axis_at, blocks in pieces:
        draws = jax.random.uniform(jax.random.fold_in(jax.random.fold_in(own_key, 6), axis_at), (blocks,), jnp.float32, least / len(pieces), high / len(pieces))
        level = level * jnp.repeat(jnp.exp(draws), extent[axis_at] // blocks).reshape((-1,) + (1,) * (len(extent) - 1 - axis_at))
    return level


def length_profile(amount, total, bound, slope):
    portions = [(1 << 20) // math.isqrt(standing ** slope) + 1 for standing in range(2, amount + 1)]
    spare, holding = total - bound - (amount - 1), [1] * (amount - 1)
    while spare > 0:
        movable = [i for i in range(amount - 1) if holding[i] < bound]
        pool, left = sum([portions[i] for i in movable]), spare
        for i in movable:
            addition = min(bound - holding[i], max(1, left * portions[i] // pool), spare)
            holding[i] = holding[i] + addition
            spare = spare - addition
    return np.array([bound] + holding)


def ragged_sizes(own_key, number_of, total, bound, lean):
    if number_of == 2:
        one = jax.random.randint(own_key, (), max(1, total - bound), min(bound, total - 1) + 1)
        return jnp.stack([one, total - one])
    sizes = jnp.asarray(length_profile(number_of, total, bound, lean), jnp.int32)
    couples = (number_of - 1) // 2
    source_of, taker = sizes[1:1 + 2 * couples:2], sizes[2:2 + 2 * couples:2]
    margin = jnp.minimum(source_of - 1, bound - taker)
    moved = jax.random.randint(jax.random.fold_in(own_key, 1), (couples,), 0, 1 << 20) % (margin + 1)
    sizes = sizes.at[1:1 + 2 * couples:2].set(source_of - moved).at[2:2 + 2 * couples:2].set(taker + moved)
    return sizes[jax.random.permutation(jax.random.fold_in(own_key, 2), number_of)]


def assign_block(key, own, number, rows, number_of, top, reach, slope):
    sequence = jax.random.permutation(key, number_of)
    packed, common = portions_of(number_of, rows * top, reach, slope, True), portions_of(number_of, rows * top, reach, slope, False)
    places = jnp.arange(number_of)

    def named(sizes, turn):
        used = int((sizes > 0).sum())
        fixed = max(1, used // 4)
        shifted = fixed + (places - fixed + turn * (used - fixed)) % max(1, number_of - fixed)
        return jnp.zeros((number_of,), jnp.int32).at[sequence[jnp.where(places < fixed, places, shifted)]].set(jnp.asarray(sizes, jnp.int32))

    sizes = jnp.where(number % 4 == 0, named(packed, number // 4), named(common, number - number // 4 - 1))
    mixed = jax.random.permutation(jax.random.fold_in(own, 3), number_of)
    giver, receiver = mixed[0:number_of // 2 * 2:2], mixed[1:number_of // 2 * 2:2]
    room = jnp.minimum(sizes[giver] - 1, reach - sizes[receiver]) // 2
    room = jnp.where((giver == sequence[0]) | (receiver == sequence[0]) | (sizes[receiver] == 0), 0, jnp.maximum(room, 0))
    shifted = jax.random.randint(jax.random.fold_in(own, 4), (number_of // 2,), 0, 1 << 20) % (room + 1)
    sizes = sizes.at[giver].add(-shifted).at[receiver].add(shifted)
    labels = jnp.searchsorted(jnp.cumsum(sizes), jnp.arange(rows * top), side="right").astype(jnp.int32)
    table = labels.reshape(top, rows).T
    table = table[jax.random.permutation(jax.random.fold_in(own, 1), rows)]
    turn = jax.random.randint(jax.random.fold_in(own, 2), (rows, 1), 0, top)
    return jnp.take_along_axis(table, (jnp.arange(top)[None, :] + turn) % top, axis=1)


def portions_of(count, total, limit, skew, full):
    loads = [(1 << 20) // math.isqrt(standing ** skew) + 1 for standing in range(1, count + 1)]
    largest = limit if full else min(limit, max(-(-total // count), total * loads[0] // sum(loads)))
    least = 1 if total - largest >= count - 1 else 0
    counts, surplus = [largest] + [least] * (count - 1), total - largest - least * (count - 1)
    while surplus > 0:
        movable = [i for i in range(1, count) if counts[i] < largest] or [i for i in range(1, count) if counts[i] < limit]
        pool, left = sum([loads[i] for i in movable]), surplus
        for i in movable:
            extra = min(limit - counts[i], max(1, left * loads[i] // pool), surplus)
            counts[i] = counts[i] + extra
            surplus = surplus - extra
    return np.array(counts)


def bell_draw(own_key, shape, width, most, split=(), held_as=jnp.bfloat16):
    drawn = width * jax.random.normal(own_key, shape, jnp.float32)
    if split:
        drawn = drawn * steps_of(own_key, shape, split, -0.22, 0.18)
    return jnp.clip(drawn, -most, most).astype(held_as)


def setup_inputs(seed: int = 0, part: int = 0) -> dict:
    streams_of = jax.random.split(jax.random.key(seed), 15)
    part_keys = jax.random.split(jax.random.fold_in(streams_of[14], part), 15)
    tokens = bell_draw(part_keys[0], (SEQ, D), 1.0, 6.0, ((0, 16),))
    lengths = ragged_sizes(part_keys[1], DOCS, SEQ, 3 * SEQ // 4, 2).astype(jnp.int32)
    attn_gain = jnp.clip(1.0 + 0.18 * jax.random.normal(streams_of[2], (D,), jnp.float32), 0.1, 1.9)
    w_query = draw_w_query(jax.random.fold_in(streams_of[14], 71), part)
    w_key = draw_w_key(jax.random.fold_in(streams_of[14], 71), part)
    w_value = bell_draw(streams_of[5], (D, KV * HD), D ** -0.5, 0.109375)
    sinks = jnp.clip(jax.random.uniform(streams_of[6], (HEADS,), jnp.float32, -2.0, 4.0), -2.0, 4.0)
    w_out = bell_draw(streams_of[7], (HEADS * HD, D), (HEADS * HD // 16) ** -0.5, 0.5, ((0, 16),))
    moe_gain = jnp.clip(1.0 + 0.18 * jax.random.normal(streams_of[8], (D,), jnp.float32), 0.1, 1.9)
    routes_keys = jax.random.split(jax.random.fold_in(part_keys[9], 1), SEQ // TOK_DEV)
    routes_turns = jax.random.permutation(jax.random.fold_in(part_keys[9], 3), SEQ // TOK_DEV)
    routes = jax.vmap(lambda own, number: assign_block(jax.random.fold_in(part_keys[9], 2), own, number, TOK_DEV, EXPERTS, TOP, CAP, 1))(routes_keys, routes_turns).reshape((SEQ, TOP))
    route_weights = jnp.clip(jnp.exp(math.log(1.0) - 2.9957323 * jax.random.uniform(part_keys[10], (SEQ, TOP), jnp.float32) ** steps_of(part_keys[10], (SEQ, TOP), ((0, 16),), -0.2, 0.2)), 0.05, 1.0)
    w_gate = bell_draw(streams_of[11], (SLABS, D, FF_SLAB), D ** -0.5, 0.109375, ((0, 16),))
    w_up = bell_draw(streams_of[12], (SLABS, D, FF_SLAB), D ** -0.5, 0.109375, ((0, 16),))
    w_down = bell_draw(streams_of[13], (SLABS, FF_SLAB, D), FF ** -0.5, 0.15625, ((0, 16),))
    return dict(tokens=tokens, lengths=lengths, attn_gain=attn_gain, w_query=w_query, w_key=w_key, w_value=w_value, sinks=sinks, w_out=w_out, moe_gain=moe_gain, routes=routes, route_weights=route_weights, w_gate=w_gate, w_up=w_up, w_down=w_down)


EPS = 1e-05
THETA = 150000.0
ALPHA = 1.702
SCALE = 0.125
NEGATIVE = -1e+30

def rms_scale(values, gain_vec):
    wide = values.astype(jnp.float32)
    inverse = lax.rsqrt(lax.optimization_barrier(jnp.mean(wide * wide, axis=-1, keepdims=True)) + EPS)
    return (wide * inverse * gain_vec.astype(jnp.float32)).astype(jnp.bfloat16)

def rotate(values, positions):
    half_size = values.shape[-1] // 2
    freqs = THETA ** (-jnp.arange(half_size, dtype=jnp.float32) / half_size)
    angles = positions.astype(jnp.float32)[:, None] * freqs[None, :]
    cosine = jnp.cos(angles)[:, None, :]
    sine = jnp.sin(angles)[:, None, :]
    first = values[..., :half_size]
    second = values[..., half_size:]
    return jnp.concatenate([first * cosine - second * sine, second * cosine + first * sine], axis=-1)

def segment_of(positions, doc_ends):
    return lax.optimization_barrier(jnp.sum((positions[:, None] >= doc_ends[None, :]).astype(jnp.int32), axis=1)).astype(jnp.int32)

def expert_rows(inputs, gate_mat, up_mat, down_mat):
    gate_val = jnp.dot(inputs, gate_mat, preferred_element_type=jnp.float32)
    up_val = jnp.dot(inputs, up_mat, preferred_element_type=jnp.float32)
    hidden = ((up_val + 1.0) * gate_val * jax.nn.sigmoid(ALPHA * gate_val)).astype(jnp.bfloat16)
    return jnp.dot(hidden, down_mat, preferred_element_type=jnp.float32).astype(jnp.bfloat16)

def reference(tokens, lengths, attn_gain, w_query, w_key, w_value, sinks, w_out, moe_gain, routes, route_weights, w_gate, w_up, w_down):
    seq_len = tokens.shape[0]
    group_size = HEADS // KV
    positions = jnp.arange(seq_len, dtype=jnp.int32)
    doc_ends = jnp.cumsum(lengths).astype(jnp.int32)
    segment = segment_of(positions, doc_ends)
    normed = rms_scale(tokens, attn_gain)
    raw_query = jnp.dot(normed, w_query, preferred_element_type=jnp.float32).reshape(seq_len, HEADS, HD)
    raw_key = jnp.dot(normed, w_key, preferred_element_type=jnp.float32).reshape(seq_len, KV, HD)
    val_rot = jnp.dot(normed, w_value, preferred_element_type=jnp.float32).astype(jnp.bfloat16).reshape(seq_len, KV, HD)
    queries = rotate(raw_query, positions).astype(jnp.bfloat16)
    key_rot = rotate(raw_key, positions).astype(jnp.bfloat16)
    allowed = (segment[:, None] == segment[None, :]) & (positions[None, :] <= positions[:, None])

    def one_head(head_id):
        q_head = lax.dynamic_index_in_dim(queries, head_id, 1, keepdims=False)
        k_head = lax.dynamic_index_in_dim(key_rot, head_id // group_size, 1, keepdims=False)
        v_head = lax.dynamic_index_in_dim(val_rot, head_id // group_size, 1, keepdims=False)
        sink_val = lax.dynamic_index_in_dim(sinks, head_id, 0, keepdims=False)
        scores = jnp.dot(q_head, k_head.T, preferred_element_type=jnp.float32) * SCALE
        scores = jnp.where(allowed, scores, NEGATIVE)
        top_val = jnp.maximum(lax.optimization_barrier(jnp.max(scores, axis=1)), sink_val)
        weights = jnp.exp(scores - top_val[:, None])
        denom = lax.optimization_barrier(jnp.sum(weights, axis=1)) + jnp.exp(sink_val - top_val)
        probs = (weights / denom[:, None]).astype(jnp.bfloat16)
        return jnp.dot(probs, v_head, preferred_element_type=jnp.float32).astype(jnp.bfloat16)
    per_head = lax.map(one_head, jnp.arange(HEADS, dtype=jnp.int32))
    attended = jnp.transpose(per_head, (1, 0, 2)).reshape(seq_len, HEADS * HD)
    mixed = (tokens.astype(jnp.float32) + jnp.dot(attended, w_out, preferred_element_type=jnp.float32)).astype(jnp.bfloat16)
    expert_in = rms_scale(mixed, moe_gain)
    block_routes = routes.reshape(N_CTX, TOK_DEV * TOP)
    onehot = (block_routes[..., None] == jnp.arange(EXPERTS, dtype=jnp.int32)[None, None, :]).astype(jnp.int32)
    slots = lax.optimization_barrier(jnp.sum((jnp.cumsum(onehot, axis=1).astype(jnp.int32) - 1) * onehot, axis=2)).astype(jnp.int32)
    block_ids = jnp.arange(N_CTX, dtype=jnp.int32)[:, None]
    row_index = (block_ids * CAP + slots).reshape(-1)
    token_ids = (block_ids * TOK_DEV + jnp.arange(TOK_DEV * TOP, dtype=jnp.int32)[None, :] // TOP).reshape(-1)
    expert_ids = block_routes.reshape(-1)
    buffer = jnp.zeros((EXPERTS, N_CTX * CAP, D), jnp.bfloat16).at[expert_ids, row_index].set(expert_in[token_ids])

    def slab_out(slab_id):
        rows_in = lax.dynamic_index_in_dim(buffer, slab_id // SPLITS, 0, keepdims=False)
        return expert_rows(rows_in, w_gate[slab_id], w_up[slab_id], w_down[slab_id])
    partials = lax.map(slab_out, jnp.arange(SLABS, dtype=jnp.int32))
    summed = lax.optimization_barrier(jnp.sum(partials.reshape(EXPERTS, SPLITS, N_CTX * CAP, D).astype(jnp.float32), axis=1)).astype(jnp.bfloat16)
    summed = lax.optimization_barrier(summed).astype(jnp.float32)
    picked = summed[expert_ids, row_index].reshape(seq_len, TOP, D)
    expert_sum = lax.optimization_barrier(jnp.sum(picked * route_weights[..., None], axis=1))
    return (mixed.astype(jnp.float32) + expert_sum).astype(jnp.bfloat16)
```

```python
import jax
import jax.numpy as jnp
from jax import lax
from jax.experimental import pallas as pl
from jax.experimental.pallas import tpu as pltpu
from jax.sharding import PartitionSpec as P

HD = 64
SPLITS = 2
TOP = 4
PLANE = 4
ORDER = (0, 2, 1, 3)

EPS = 1e-05
THETA = 150000.0
ALPHA = 1.702
SCALE = 0.125
NEGATIVE = -1e30
HIDDEN_BLOCK = 256


def swap_with(x, axis, bits):
    return lax.ppermute(x, axis, [(i, i ^ bits) for i in range(lax.axis_size(axis))])


def after(value, *earlier):
    return lax.optimization_barrier((value, *earlier))[0]


def over_planes(block, planes):
    held = {0: block}
    bit = planes // 2
    while bit:
        for k in sorted(held):
            held[k ^ bit] = swap_with(held[k], "ctx", PLANE * bit)
        bit //= 2
    return held


def rms_scale(values, gain_vec):
    wide = values.astype(jnp.float32)
    inverse = lax.rsqrt(jnp.mean(wide * wide, axis=-1, keepdims=True) + EPS)
    return (wide * inverse * gain_vec).astype(jnp.bfloat16)


def angle_tables(positions):
    half_size = HD // 2
    freqs = THETA ** (-jnp.arange(half_size, dtype=jnp.float32) / half_size)
    angles = positions.astype(jnp.float32)[:, None] * jnp.tile(freqs, 4)[None, :]
    sign = jnp.tile(jnp.repeat(jnp.array([-1.0, 1.0], jnp.float32), half_size), 2)
    return jnp.cos(angles), jnp.sin(angles) * sign


def rotate_key(values, cosine, sine):
    rows, cols = values.shape
    pieces = values.reshape(rows, cols // HD, 2, HD // 2)
    turned = pieces[:, :, ::-1, :].reshape(rows, cols)
    reps = cols // cosine.shape[1]
    return (values * jnp.tile(cosine, (1, reps)) + turned * jnp.tile(sine, (1, reps))).astype(
        jnp.bfloat16
    )


def attention_kernel(planes, kv_heads, rows_of, info, lo_first, sink_ref, nb_ref, cos_ref, sin_ref,
                     lo_ref, pos_ref, own_kv, y_kv, c_kv, *rest):
    weights = rest[: 2 * planes]
    out_ref = rest[2 * planes]
    q_ref, bias_ref, max_ref, acc_ref = rest[2 * planes + 1:]
    me, half = info[0], info[1]
    plane = me // PLANE
    rows = PLANE * rows_of
    width = 2 * HD
    total = jnp.zeros((rows, kv_heads * width), jnp.float32)
    for k in range(planes):
        for side in range(2):
            part = weights[2 * k + side]
            chosen = half if side == 0 else 1 - half
            for piece in range(2):
                device = me ^ (PLANE * k + 2 * chosen + piece)
                total += jnp.dot(nb_ref[device], part[piece], preferred_element_type=jnp.float32)
    lane = lax.broadcasted_iota(jnp.int32, (rows, width), 1)
    low_half = lane < HD
    first = lane % HD < HD // 2
    for g in range(kv_heads):
        tile = total[:, g * width:(g + 1) * width]
        turned = jnp.where(first, pltpu.roll(tile, width - HD // 2, 1), pltpu.roll(tile, HD // 2, 1))
        tile = (tile * cos_ref[...] + turned * sin_ref[...]) * SCALE
        moved = pltpu.roll(tile, HD, 1)
        if g % 2 == 0:
            heads = (jnp.where(low_half, tile, 0.0), jnp.where(low_half, moved, 0.0))
        else:
            heads = (jnp.where(low_half, 0.0, moved), jnp.where(low_half, 0.0, tile))
        for u in range(2):
            for m in range(PLANE):
                q_ref[g, m, u * rows_of:(u + 1) * rows_of, :] = heads[u][
                    m * rows_of:(m + 1) * rows_of
                ].astype(jnp.bfloat16)

    key_iota = lax.broadcasted_iota(jnp.int32, (1, rows_of), 1)
    for k in range(planes):
        @pl.when((plane ^ k) <= plane)
        def _():
            key_pos = jnp.concatenate(
                [(me ^ (PLANE * k + m)) * rows_of + key_iota for m in ORDER], axis=1
            )
            allowed = (key_pos >= lo_ref[...]) & (key_pos <= pos_ref[...])
            bias_ref[k] = jnp.where(allowed, 0.0, NEGATIVE)

    def chunk(k, lanes):
        at = pl.ds(k * rows_of, rows_of)
        late = pl.ds((planes + k) * rows_of, rows_of)
        return jnp.concatenate(
            [own_kv[at, lanes], y_kv[at, lanes], c_kv[at, lanes], c_kv[late, lanes]], axis=0
        )

    lane_q = lax.broadcasted_iota(jnp.int32, (2 * rows_of, width), 1) < HD
    lane_k = lax.broadcasted_iota(jnp.int32, (rows, width), 1) < HD
    row_q = lax.broadcasted_iota(jnp.int32, (2 * rows_of, width), 0) < rows_of
    for g in range(kv_heads):
        mine = lane_q if g % 2 == 0 else ~lane_q
        mine_k = lane_k if g % 2 == 0 else ~lane_k
        key_lanes = pl.ds((g // 2) * width, width)
        val_lanes = pl.ds((kv_heads // 2 + g // 2) * width, width)

        def q_block(m, carry):
            max_ref[...] = jnp.where(row_q, sink_ref[2 * g], sink_ref[2 * g + 1])
            acc_ref[...] = jnp.where(mine, 0.0, 1.0)
            for k in range(planes):
                last_key = ((plane ^ k) + 1) * rows - 1

                @pl.when(((plane ^ k) <= plane) & (lo_first[m] <= last_key))
                def _():
                    scores = lax.dot_general(
                        q_ref[g, m], chunk(k, key_lanes), (((1,), (1,)), ((), ())),
                        preferred_element_type=jnp.float32,
                    )
                    bias = bias_ref[k, pl.ds(pl.multiple_of(m * rows_of, rows_of), rows_of), :]
                    scores = (scores.reshape(2, rows_of, rows) + bias[None]).reshape(
                        2 * rows_of, rows
                    )
                    old = max_ref[...]
                    new = jnp.maximum(old, jnp.max(scores, axis=1, keepdims=True))
                    max_ref[...] = new
                    probs = jnp.exp(scores - new[:, :1]).astype(jnp.bfloat16)
                    vals = jnp.where(mine_k, chunk(k, val_lanes), jnp.bfloat16(1.0))
                    acc_ref[...] = acc_ref[...] * jnp.exp(old - new) + jnp.dot(
                        probs, vals, preferred_element_type=jnp.float32
                    )
            acc = acc_ref[...]
            done = acc / pltpu.roll(acc, HD, 1)
            one, two = done[:rows_of], done[rows_of:]
            low = lane_q[:rows_of]
            if g % 2 == 0:
                both = jnp.where(low, one, pltpu.roll(two, HD, 1))
            else:
                both = jnp.where(low, pltpu.roll(one, HD, 1), two)
            out_ref[pl.ds(pl.multiple_of(m * rows_of, rows_of), rows_of),
                    g * width:(g + 1) * width] = both.astype(jnp.bfloat16)
            return carry

        lax.fori_loop(0, PLANE, q_block, 0)


def attend(info, lo_first, sinks, nb, cosine, sine, lo, pos, own_kv, y_kv, c_kv, weights, planes):
    kv_heads = own_kv.shape[1] // (2 * HD)
    rows = cosine.shape[0]
    rows_of = rows // PLANE
    smem = pl.BlockSpec(memory_space=pltpu.SMEM)
    vmem = pl.BlockSpec(memory_space=pltpu.VMEM)
    operands = (info, lo_first, sinks, nb, cosine, sine, lo, pos, own_kv, y_kv, c_kv, *weights)

    def body(*refs):
        attention_kernel(planes, kv_heads, rows_of, *refs)

    return pl.pallas_call(
        body,
        out_shape=jax.ShapeDtypeStruct((rows, kv_heads * 2 * HD), jnp.bfloat16),
        in_specs=[smem] * 3 + [vmem] * (len(operands) - 3),
        out_specs=vmem,
        scratch_shapes=[
            pltpu.VMEM((kv_heads, PLANE, 2 * rows_of, 2 * HD), jnp.bfloat16),
            pltpu.VMEM((planes, rows, rows), jnp.float32),
            pltpu.VMEM((2 * rows_of, 2 * HD), jnp.float32),
            pltpu.VMEM((2 * rows_of, 2 * HD), jnp.float32),
        ],
        compiler_params=pltpu.CompilerParams(vmem_limit_bytes=50 * 1024 * 1024),
        cost_estimate=pl.CostEstimate(
            flops=12_000_000_000, bytes_accessed=12_000_000, transcendentals=8_000_000
        ),
    )(*operands)


def expert_kernel(steps, x_ref, row_ref, gate_a, up_a, down_a, gate_b, up_b, down_b, out_ref, acc_ref):
    step = pl.program_id(0)

    @pl.when(step == 0)
    def _():
        acc_ref[...] = jnp.zeros_like(acc_ref)

    def add(gate, up, down):
        x = x_ref[...]
        gate_val = jnp.dot(x, gate[0], preferred_element_type=jnp.float32)
        up_val = jnp.dot(x, up[0], preferred_element_type=jnp.float32)
        hidden = ((up_val + 1.0) * gate_val * jax.nn.sigmoid(ALPHA * gate_val)).astype(jnp.bfloat16)
        acc_ref[...] += jnp.dot(hidden, down[0], preferred_element_type=jnp.float32)

    @pl.when(step < steps)
    def _():
        add(gate_a, up_a, down_a)

    @pl.when(step >= steps)
    def _():
        add(gate_b, up_b, down_b)

    @pl.when(step == 2 * steps - 1)
    def _():
        out_ref[...] = (acc_ref[...] * row_ref[...]).astype(jnp.bfloat16)


def expert(x, row_weights, own, mate):
    rows, width = x.shape
    hidden = own[0].shape[2]
    steps = hidden // HIDDEN_BLOCK

    def early(i):
        return jnp.minimum(i, steps - 1)

    def late(i):
        return jnp.maximum(i - steps, 0)

    def specs(place):
        return [
            pl.BlockSpec((1, width, HIDDEN_BLOCK), lambda i: (0, 0, place(i))),
            pl.BlockSpec((1, width, HIDDEN_BLOCK), lambda i: (0, 0, place(i))),
            pl.BlockSpec((1, HIDDEN_BLOCK, width), lambda i: (0, place(i), 0)),
        ]

    def body(*refs):
        expert_kernel(steps, *refs)

    return pl.pallas_call(
        body,
        grid=(2 * steps,),
        out_shape=jax.ShapeDtypeStruct((rows, width), jnp.bfloat16),
        in_specs=[
            pl.BlockSpec((rows, width), lambda i: (0, 0)),
            pl.BlockSpec((rows, 1), lambda i: (0, 0)),
            *specs(early),
            *specs(late),
        ],
        out_specs=pl.BlockSpec((rows, width), lambda i: (0, 0)),
        scratch_shapes=[pltpu.VMEM((rows, width), jnp.float32)],
        compiler_params=pltpu.CompilerParams(vmem_limit_bytes=50 * 1024 * 1024),
        cost_estimate=pl.CostEstimate(
            flops=12 * rows * width * hidden,
            bytes_accessed=12 * width * hidden,
            transcendentals=2 * rows * hidden,
        ),
    )(x, row_weights, *own, *mate)


def per_device(
    tokens,
    lengths,
    attn_gain,
    w_query,
    w_key,
    w_value,
    sinks,
    w_out,
    moe_gain,
    routes,
    route_weights,
    w_gate,
    w_up,
    w_down,
):
    tok_rows, model_width = tokens.shape
    devices = lax.axis_size("ctx")
    planes = devices // PLANE
    me = lax.axis_index("ctx")
    in_plane = me % PLANE
    half = lax.axis_index("groups") % 2
    cols = w_query.shape[1] // devices
    q_rows = w_query.shape[0]

    w_parts = jnp.stack(
        [
            jnp.concatenate(
                [
                    w_query[:, (PLANE * zz + j) * cols:(PLANE * zz + j + 1) * cols]
                    for zz in range(planes)
                ],
                axis=1,
            )
            for j in range(PLANE)
        ]
    )
    w_got = [lax.dynamic_index_in_dim(w_parts, in_plane, 0, keepdims=False)]
    for m in (1, 2, 3):
        piece = lax.dynamic_index_in_dim(w_parts, in_plane ^ m, 0, keepdims=False)
        w_got.append(swap_with(piece, "ctx", m))
    w_low = jnp.stack(w_got[:2])
    w_high = jnp.stack(w_got[2:])
    w_mine = jnp.where(half == 0, w_low, w_high)
    w_rest = jnp.where(half == 0, w_high, w_low)
    mine_of = over_planes(w_mine, planes)
    q_weights = [w_mine, w_rest]
    for k in range(1, planes):
        q_weights += [mine_of[k], swap_with(mine_of[k], "groups", 1)]

    normed = rms_scale(tokens, attn_gain)
    two = jnp.concatenate([normed, swap_with(normed, "ctx", 2)], axis=0)
    plane_tokens = jnp.concatenate([two, swap_with(two, "ctx", 1)], axis=0)
    nb = jnp.stack([plane_tokens[:, b * q_rows:(b + 1) * q_rows] for b in range(devices)])

    span = jnp.arange(tok_rows, dtype=jnp.int32)
    positions = jnp.concatenate([(me ^ m) * tok_rows + span for m in ORDER])
    cosine, sine = angle_tables(positions)
    raw_key = jnp.dot(normed, w_key, preferred_element_type=jnp.float32)
    val_flat = jnp.dot(normed, w_value, preferred_element_type=jnp.float32).astype(jnp.bfloat16)
    key_flat = rotate_key(raw_key, cosine[:tok_rows], sine[:tok_rows])
    kv_of = over_planes(jnp.concatenate([key_flat, val_flat], axis=1), planes)
    own_kv = jnp.concatenate([kv_of[k] for k in range(planes)], axis=0)
    y_kv = swap_with(own_kv, "ctx", 2)
    c_kv = swap_with(jnp.concatenate([own_kv, y_kv], axis=0), "ctx", 1)

    wo_halves = w_out.reshape(2, w_out.shape[0] // 2, model_width)
    wo_mine = lax.dynamic_index_in_dim(wo_halves, half, 0, keepdims=False)
    wo_of = over_planes(after(wo_mine, mine_of[planes - 1]), planes)
    plane = me // PLANE
    wo = jnp.zeros((planes, 2) + wo_mine.shape, jnp.bfloat16)
    wo = lax.dynamic_update_slice(wo, wo_halves[None], (plane, 0, 0, 0))
    for k in range(1, planes):
        other = swap_with(wo_of[k], "groups", 1)
        wo = lax.dynamic_update_slice(wo, wo_of[k][None, None], (plane ^ k, half, 0, 0))
        wo = lax.dynamic_update_slice(wo, other[None, None], (plane ^ k, 1 - half, 0, 0))
    wo = wo.reshape(-1, model_width)

    own_slab = (w_gate, w_up, w_down)
    mate_slab = tuple(swap_with(after(w, w_mine, plane_tokens), "ctx", 1) for w in own_slab)

    experts_num = devices // SPLITS
    capacity = tok_rows * TOP * 17 // (16 * experts_num)
    padded = -(-capacity // 8) * 8
    facts = lax.all_gather(
        jnp.concatenate([routes.astype(jnp.float32), route_weights], axis=1), "ctx", axis=0
    )
    mine_expert = (me // SPLITS).astype(jnp.float32)
    other_expert = ((me // SPLITS) ^ 1).astype(jnp.float32)
    earlier = (span[:, None] < span[None, :]).astype(jnp.bfloat16)
    slot_ids = jnp.arange(padded, dtype=jnp.float32)

    def chosen_rows(columns, expert_id):
        block = jnp.stack(
            [
                lax.dynamic_index_in_dim(facts, me ^ (columns + PLANE * k), 0, keepdims=False)
                for k in range(planes)
            ]
        )
        match = block[:, :, :TOP] == expert_id
        hit = jnp.any(match, axis=2)
        weight = jnp.sum(jnp.where(match, block[:, :, TOP:], 0.0), axis=2)
        slot = jnp.dot(hit.astype(jnp.bfloat16), earlier, preferred_element_type=jnp.float32)
        pick = hit[:, None, :] & (slot[:, None, :] == slot_ids[None, :, None])
        row_weight = jnp.sum(jnp.where(pick, weight[:, None, :], 0.0), axis=2)
        return pick.astype(jnp.bfloat16), row_weight

    pick_own, weight_own = chosen_rows(0, mine_expert)
    pick_other, _ = chosen_rows(0, other_expert)
    _, weight_far = chosen_rows(2, mine_expert)

    doc_ends = jnp.cumsum(lengths)
    lo = jnp.max(jnp.where(doc_ends[None, :] <= positions[:, None], doc_ends[None, :], 0), axis=1)
    heads_of = cols // HD
    my_sinks = lax.dynamic_index_in_dim(
        sinks.reshape(planes, PLANE, heads_of), in_plane, 1, keepdims=False
    ).reshape(-1)
    info = jnp.stack([me, half]).astype(jnp.int32)
    attended = attend(
        info, lo[::tok_rows], my_sinks, nb, cosine, sine, lo[:, None], positions[:, None],
        own_kv, y_kv, c_kv, q_weights, planes,
    )
    partial = jnp.dot(attended, wo, preferred_element_type=jnp.float32)
    wide = 2 * tok_rows
    from_core = swap_with(partial[wide:].astype(jnp.bfloat16), "ctx", 1)
    summed = partial[:wide] + from_core.astype(jnp.float32)
    from_y = swap_with(summed[tok_rows:].astype(jnp.bfloat16), "ctx", 2)
    mixed = (
        tokens.astype(jnp.float32) + summed[:tok_rows] + from_y.astype(jnp.float32)
    ).astype(jnp.bfloat16)
    expert_in = rms_scale(mixed, moe_gain)

    blocks = over_planes(expert_in, planes)

    def rows_for(pick, k):
        return jnp.dot(pick[k], blocks[k], preferred_element_type=jnp.float32).astype(jnp.bfloat16)

    def run(ks):
        far = [swap_with(rows_for(pick_other, k), "ctx", 2) for k in ks]
        near = [rows_for(pick_own, k) for k in ks]
        weights = jnp.concatenate([weight_own[k] for k in ks] + [weight_far[k] for k in ks])
        out = expert(jnp.concatenate(near + far, axis=0), weights[:, None], own_slab, mate_slab)
        cut = len(ks) * padded
        back = swap_with(out[cut:], "ctx", 2)
        return {
            k: lax.dot_general(
                pick_own[k], out[i * padded:(i + 1) * padded], (((0,), (0,)), ((), ())),
                preferred_element_type=jnp.float32,
            )
            + lax.dot_general(
                pick_other[k], back[i * padded:(i + 1) * padded], (((0,), (0,)), ((), ())),
                preferred_element_type=jnp.float32,
            )
            for i, k in enumerate(ks)
        }

    sums = run(list(range(planes - 1)))
    sums.update(run([planes - 1]))
    bit = 1
    while bit < planes:
        for k in sorted(sums, reverse=True):
            if k & bit:
                got = swap_with(sums.pop(k).astype(jnp.bfloat16), "ctx", PLANE * bit)
                sums[k ^ bit] = sums[k ^ bit] + got.astype(jnp.float32)
        bit *= 2
    return (mixed.astype(jnp.float32) + sums[0]).astype(jnp.bfloat16)


def solution(mesh):
    placed = (
        P(("groups", "ctx"), None),
        P("groups"),
        P(),
        P("ctx", None),
        P(),
        P(),
        P(),
        P("ctx", None),
        P(),
        P(("groups", "ctx"), None),
        P(("groups", "ctx"), None),
        P("ctx", None, None),
        P("ctx", None, None),
        P("ctx", None, None),
    )
    return jax.shard_map(
        per_device,
        mesh=mesh,
        in_specs=placed,
        out_specs=P(("groups", "ctx"), None),
        check_vma=False,
    )
```

```python
import jax
import jax.numpy as jnp
from jax import lax
from jax.experimental import pallas as pl
from jax.experimental.pallas import tpu as pltpu
from jax.sharding import PartitionSpec as P

HD = 64
SPLITS = 2
TOP = 4
PLANE = 4
ORDER = (0, 2, 1, 3)

EPS = 1e-05
THETA = 150000.0
ALPHA = 1.702
SCALE = 0.125
NEGATIVE = -1e30


def swap_with(x, axis, bits):
    return lax.ppermute(x, axis, [(i, i ^ bits) for i in range(lax.axis_size(axis))])


def after(value, *earlier):
    return lax.optimization_barrier((value, *earlier))[0]


def over_planes(block, planes, gates=()):
    held = {0: block}
    bit = planes // 2
    while bit:
        for k in sorted(held, reverse=True):
            own = held[k]
            if k == 0 and gates:
                own = after(own, gates[0 if bit == planes // 2 else 1])
            held[k ^ bit] = swap_with(own, "ctx", PLANE * bit)
        bit //= 2
    return held


def lane_padded(width):
    return -(-width // 128) * 128


def rms_scale(values, gain_vec):
    wide = values.astype(jnp.float32)
    inverse = lax.rsqrt(jnp.mean(wide * wide, axis=-1, keepdims=True) + EPS)
    return (wide * inverse * gain_vec).astype(jnp.bfloat16)


def angle_tables(positions):
    half_size = HD // 2
    freqs = THETA ** (-jnp.arange(half_size, dtype=jnp.float32) / half_size)
    angles = positions.astype(jnp.float32)[:, None] * jnp.tile(freqs, 4)[None, :]
    sign = jnp.tile(jnp.repeat(jnp.array([-1.0, 1.0], jnp.float32), half_size), 2)
    return jnp.cos(angles), jnp.sin(angles) * sign


def rotate_key(values, cosine, sine):
    rows, cols = values.shape
    pieces = values.reshape(rows, cols // HD, 2, HD // 2)
    turned = pieces[:, :, ::-1, :].reshape(rows, cols)
    reps = cols // cosine.shape[1]
    return (values * jnp.tile(cosine, (1, reps)) + turned * jnp.tile(sine, (1, reps))).astype(
        jnp.bfloat16
    )


def whole_call(body, out_shapes, operands, scalars=1, scratch=(), limit=24, flops=0):
    smem = pl.BlockSpec(memory_space=pltpu.SMEM)
    vmem = pl.BlockSpec(memory_space=pltpu.VMEM)
    size = sum(x.size * x.dtype.itemsize for x in operands)
    return pl.pallas_call(
        body,
        out_shape=out_shapes,
        in_specs=[smem] * scalars + [vmem] * (len(operands) - scalars),
        out_specs=jax.tree.map(lambda _: vmem, out_shapes),
        scratch_shapes=list(scratch),
        compiler_params=pltpu.CompilerParams(vmem_limit_bytes=limit * 1024 * 1024),
        cost_estimate=pl.CostEstimate(flops=flops, bytes_accessed=size, transcendentals=0),
    )(*operands)


def split_query(info, w_query, planes):
    rows = w_query.shape[0]
    cols = w_query.shape[1] // (planes * PLANE)
    if cols % 128:
        in_plane = info[0] % PLANE
        parts = jnp.stack(
            [
                jnp.concatenate(
                    [
                        w_query[:, (PLANE * zz + j) * cols:(PLANE * zz + j + 1) * cols]
                        for zz in range(planes)
                    ],
                    axis=1,
                )
                for j in range(PLANE)
            ]
        )
        return [
            lax.dynamic_index_in_dim(parts, in_plane ^ m, 0, keepdims=False) for m in range(PLANE)
        ]

    def body(info_ref, w_ref, *outs):
        in_plane = info_ref[0] % PLANE
        for m in range(PLANE):
            for zz in range(planes):
                start = pl.multiple_of((PLANE * zz + (in_plane ^ m)) * cols, 128)
                outs[m][:, zz * cols:(zz + 1) * cols] = w_ref[:, pl.ds(start, cols)]

    shape = jax.ShapeDtypeStruct((rows, planes * cols), jnp.bfloat16)
    return whole_call(body, [shape] * PLANE, (info, w_query))


def query_kernel(planes, kv_heads, rows_of, info, nb_ref, cos_ref, sin_ref, *rest):
    weights = rest[: 2 * planes]
    q_ref = rest[2 * planes]
    me, half = info[0], info[1]
    width = 2 * HD
    wide = 2 * rows_of
    lane = lax.broadcasted_iota(jnp.int32, (wide, width), 1)
    low_half = lane < HD
    first = lane % HD < HD // 2
    for r in range(2):
        total = None
        for k in range(planes):
            for side in range(2):
                chosen = half if side == 0 else 1 - half
                pair = (me ^ (PLANE * k + 2 * chosen)) // 2
                term = jnp.dot(
                    nb_ref[pair, r * wide:(r + 1) * wide, :], weights[2 * k + side][...],
                    preferred_element_type=jnp.float32,
                )
                total = term if total is None else total + term
        at = slice(r * wide, (r + 1) * wide)
        for g in range(kv_heads):
            tile = total[:, g * width:(g + 1) * width]
            turned = jnp.where(
                first, pltpu.roll(tile, width - HD // 2, 1), pltpu.roll(tile, HD // 2, 1)
            )
            tile = (tile * cos_ref[at, :] + turned * sin_ref[at, :]) * SCALE
            moved = pltpu.roll(tile, HD, 1)
            if g % 2 == 0:
                heads = (jnp.where(low_half, tile, 0.0), jnp.where(low_half, moved, 0.0))
            else:
                heads = (jnp.where(low_half, 0.0, moved), jnp.where(low_half, 0.0, tile))
            for u in range(2):
                for m in range(2):
                    start = (2 * (2 * r + m) + u) * rows_of
                    q_ref[g, start:start + rows_of, :] = heads[u][
                        m * rows_of:(m + 1) * rows_of
                    ].astype(jnp.bfloat16)


def make_queries(info, nb, cosine, sine, weights, planes, cols):
    rows = cosine.shape[0]
    kv_heads = planes * cols // (2 * HD)

    def body(*refs):
        query_kernel(planes, kv_heads, rows // PLANE, *refs)

    return whole_call(
        body,
        jax.ShapeDtypeStruct((kv_heads, 2 * rows, 2 * HD), jnp.bfloat16),
        (info, nb, cosine, sine, *weights),
        limit=32,
        flops=8_000_000_000,
    )


def attention_kernel(planes, kv_heads, rows_of, info, lo_first, sink_ref, q_ref, lo_ref, pos_ref,
                     own_kv, y_kv, c_kv, out_ref, bias_ref, score_ref, max_ref, acc_ref):
    me = info[0]
    plane = me // PLANE
    rows = PLANE * rows_of
    width = 2 * HD
    wide = 2 * rows_of
    earliest = lo_first[0]
    for m in range(1, PLANE):
        earliest = jnp.minimum(earliest, lo_first[m])
    needed = [
        ((plane ^ k) <= plane) & (earliest < ((plane ^ k) + 1) * rows) for k in range(planes)
    ]

    def where_needed(k, act):
        if k:
            pl.when(needed[k])(act)
        else:
            act()

    def chunk(k, lanes):
        at = slice(k * rows_of, (k + 1) * rows_of)
        late = slice((planes + k) * rows_of, (planes + k + 1) * rows_of)
        return jnp.concatenate(
            [own_kv[at, lanes], y_kv[at, lanes], c_kv[at, lanes], c_kv[late, lanes]], axis=0
        )

    key_iota = lax.broadcasted_iota(jnp.int32, (1, rows_of), 1)
    for k in range(planes):
        def set_bias(k=k):
            key_pos = jnp.concatenate(
                [(me ^ (PLANE * k + m)) * rows_of + key_iota for m in ORDER], axis=1
            )
            allowed = (key_pos >= lo_ref[...]) & (key_pos <= pos_ref[...])
            bias_ref[k] = jnp.where(allowed, 0.0, NEGATIVE)

        where_needed(k, set_bias)

    lane_q = lax.broadcasted_iota(jnp.int32, (wide, width), 1) < HD
    lane_k = lax.broadcasted_iota(jnp.int32, (rows, width), 1) < HD
    row_q = lax.broadcasted_iota(jnp.int32, (wide, 1), 0) < rows_of
    cols = out_ref.shape[2]
    for g in range(kv_heads):
        mine = lane_q if g % 2 == 0 else ~lane_q
        mine_k = lane_k if g % 2 == 0 else ~lane_k
        key_lanes = slice((g // 2) * width, (g // 2 + 1) * width)
        val_lanes = slice((kv_heads // 2 + g // 2) * width, (kv_heads // 2 + g // 2 + 1) * width)

        for k in range(planes):
            def scores(k=k):
                keys = chunk(k, key_lanes)
                for m in range(PLANE):
                    at = slice(m * wide, (m + 1) * wide)
                    score = lax.dot_general(
                        q_ref[g, at, :], keys, (((1,), (1,)), ((), ())),
                        preferred_element_type=jnp.float32,
                    )
                    bias = bias_ref[k, m * rows_of:(m + 1) * rows_of, :]
                    score = (score.reshape(2, rows_of, rows) + bias[None]).reshape(wide, rows)
                    score_ref[k, at, :] = score
                    top = score[:, :width]
                    for start in range(width, rows, width):
                        top = jnp.maximum(top, score[:, start:start + width])
                    max_ref[at, :] = jnp.maximum(max_ref[at, :], top) if k else top

            where_needed(k, scores)

        for m in range(PLANE):
            at = slice(m * wide, (m + 1) * wide)
            sink = jnp.where(row_q, sink_ref[2 * g], sink_ref[2 * g + 1])
            top = jnp.maximum(jnp.max(max_ref[at, :], axis=1, keepdims=True), sink)
            max_ref[at, :] = jnp.broadcast_to(top, (wide, width))
            acc_ref[at, :] = jnp.where(mine, 0.0, jnp.exp(sink - top))

        for k in range(planes):
            def gather(k=k):
                vals = jnp.where(mine_k, chunk(k, val_lanes), jnp.bfloat16(1.0))
                for m in range(PLANE):
                    at = slice(m * wide, (m + 1) * wide)
                    top = max_ref[at, :]
                    probs = jnp.concatenate(
                        [
                            jnp.exp(score_ref[k, at, start:start + width] - top).astype(jnp.bfloat16)
                            for start in range(0, rows, width)
                        ],
                        axis=1,
                    )
                    acc_ref[at, :] += jnp.dot(probs, vals, preferred_element_type=jnp.float32)

            where_needed(k, gather)

        for m in range(PLANE):
            acc = acc_ref[m * wide:(m + 1) * wide, :]
            done = acc / pltpu.roll(acc, HD, 1)
            one, two = done[:rows_of], done[rows_of:]
            low = lane_q[:rows_of]
            if g % 2 == 0:
                both = jnp.where(low, one, pltpu.roll(two, HD, 1))
            else:
                both = jnp.where(low, pltpu.roll(one, HD, 1), two)
            both = both.astype(jnp.bfloat16)
            for i in range(width // cols):
                out_ref[g * (width // cols) + i, m * rows_of:(m + 1) * rows_of, :] = both[
                    :, i * cols:(i + 1) * cols
                ]


def attend(info, lo_first, sinks, queries, lo, pos, kv, planes, cols):
    rows = pos.shape[0]
    kv_heads = queries.shape[0]

    def body(*refs):
        attention_kernel(planes, kv_heads, rows // PLANE, *refs)

    return whole_call(
        body,
        jax.ShapeDtypeStruct((planes, rows, cols), jnp.bfloat16),
        (info, lo_first, sinks, queries, lo, pos, *kv),
        scalars=3,
        scratch=[
            pltpu.VMEM((planes, rows, rows), jnp.float32),
            pltpu.VMEM((planes, 2 * rows, rows), jnp.float32),
            pltpu.VMEM((2 * rows, 2 * HD), jnp.float32),
            pltpu.VMEM((2 * rows, 2 * HD), jnp.float32),
        ],
        limit=48,
        flops=16_000_000_000,
    )


def project(info, attended, own, parts, planes):
    _, rows, cols = attended.shape
    width = own.shape[1]
    padded = lane_padded(width)
    wide = rows // 2

    def body(info_ref, att_ref, own_ref, *rest):
        pieces = rest[: 2 * (planes - 1)]
        send_ref, keep_ref, att, weight = rest[2 * (planes - 1):]
        plane, half = info_ref[0] // PLANE, info_ref[1]
        short = cols // 2
        weight[:cols, :] = own_ref[...]
        for k in range(planes):
            att[:, k * cols:(k + 1) * cols] = att_ref[plane ^ k]
            if k:
                for side in range(2):
                    chosen = half if side == 0 else 1 - half
                    at = pl.multiple_of(k * cols + chosen * short, short)
                    weight[pl.ds(at, short), :] = pieces[2 * (k - 1) + side][...]
        for start in range(0, width, 640):
            lanes = slice(start, min(width, start + 640))
            send_ref[:, lanes] = jnp.dot(
                att[wide:], weight[:, lanes], preferred_element_type=jnp.float32
            ).astype(jnp.bfloat16)
            keep_ref[:, lanes] = jnp.dot(
                att[:wide], weight[:, lanes], preferred_element_type=jnp.float32
            )
        send_ref[:, width:] = jnp.zeros((wide, padded - width), jnp.bfloat16)
        keep_ref[:, width:] = jnp.zeros((wide, padded - width), jnp.float32)

    return whole_call(
        body,
        [
            jax.ShapeDtypeStruct((wide, padded), jnp.bfloat16),
            jax.ShapeDtypeStruct((wide, padded), jnp.float32),
        ],
        (info, attended, own, *parts),
        scratch=[
            pltpu.VMEM((rows, planes * cols), jnp.bfloat16),
            pltpu.VMEM((planes * cols, width), jnp.bfloat16),
        ],
        flops=4_000_000_000,
    )


def add_core(keep, got):
    rows, width = keep.shape[0] // 2, keep.shape[1]

    def body(keep_ref, got_ref, send_ref, rest_ref):
        rest_ref[...] = keep_ref[:rows] + got_ref[:rows].astype(jnp.float32)
        send_ref[...] = (keep_ref[rows:] + got_ref[rows:].astype(jnp.float32)).astype(jnp.bfloat16)

    return whole_call(
        body,
        [
            jax.ShapeDtypeStruct((rows, width), jnp.bfloat16),
            jax.ShapeDtypeStruct((rows, width), jnp.float32),
        ],
        (keep, got),
        scalars=0,
    )


def mix(tokens, keep, got, gain):
    rows, width = tokens.shape
    padded = keep.shape[1]

    def body(tokens_ref, keep_ref, got_ref, gain_ref, mixed_ref, in_ref):
        mixed = (
            tokens_ref[...].astype(jnp.float32)
            + keep_ref[:, :width]
            + got_ref[:, :width].astype(jnp.float32)
        ).astype(jnp.bfloat16)
        mixed_ref[...] = mixed
        in_ref[:, :width] = rms_scale(mixed, gain_ref[...])
        in_ref[:, width:] = jnp.zeros((rows, padded - width), jnp.bfloat16)

    return whole_call(
        body,
        [
            jax.ShapeDtypeStruct((rows, width), jnp.bfloat16),
            jax.ShapeDtypeStruct((rows, padded), jnp.bfloat16),
        ],
        (tokens, keep, got, gain[None]),
        scalars=0,
    )


def finish(mixed, total, *got):
    rows, width = mixed.shape

    def body(mixed_ref, total_ref, *rest):
        out_ref = rest[-1]
        for start in range(0, width, 128):
            size = min(128, width - start)
            lanes = slice(start, start + size)
            value = mixed_ref[:, lanes].astype(jnp.float32) + total_ref[:, lanes]
            for ref in rest[:-1]:
                value += ref[:, lanes].astype(jnp.float32)
            if size < 128:
                value = jnp.concatenate([value, jnp.zeros((rows, 128 - size), jnp.float32)], axis=1)
            out_ref[lanes, :] = value.T[:size].astype(jnp.bfloat16)

    out = jax.ShapeDtypeStruct((width, rows), jnp.bfloat16)
    return whole_call(body, out, (mixed, total, *got), scalars=0).T


def by_columns(hidden, down):
    return lax.dot_general(hidden, down, (((1,), (1,)), ((), ())), preferred_element_type=jnp.float32)


def expert(x, row_weights, own, mate):
    rows, padded = x.shape
    width, hidden = own[0].shape[1:]

    def body(x_ref, row_ref, *rest):
        slabs, out_ref, held, sem = rest[:6], rest[6], rest[7], rest[8]
        copies = [
            pltpu.make_async_copy(slabs[i].at[0], held.at[i], sem.at[i]) for i in range(6)
        ]
        for copy in copies:
            copy.start()
        total = None
        for side in range(2):
            i = 3 * side
            inputs = x_ref[:, :width]
            copies[i].wait()
            gate_val = jnp.dot(inputs, held[i], preferred_element_type=jnp.float32)
            copies[i + 1].wait()
            up_val = jnp.dot(inputs, held[i + 1], preferred_element_type=jnp.float32)
            rows_in = ((up_val + 1.0) * gate_val * jax.nn.sigmoid(ALPHA * gate_val)).astype(
                jnp.bfloat16
            )
            copies[i + 2].wait()
            term = by_columns(rows_in, held[i + 2])
            total = term if total is None else total + term
        out_ref[:, :width] = (total * row_ref[...]).astype(jnp.bfloat16)
        out_ref[:, width:] = jnp.zeros((rows, padded - width), jnp.bfloat16)

    vmem = pl.BlockSpec(memory_space=pltpu.VMEM)
    return pl.pallas_call(
        body,
        out_shape=jax.ShapeDtypeStruct((rows, padded), jnp.bfloat16),
        in_specs=[vmem, vmem] + [pl.BlockSpec(memory_space=pl.ANY)] * 6,
        out_specs=vmem,
        scratch_shapes=[
            pltpu.VMEM((6, width, hidden), jnp.bfloat16),
            pltpu.SemaphoreType.DMA((6,)),
        ],
        compiler_params=pltpu.CompilerParams(vmem_limit_bytes=48 * 1024 * 1024),
        cost_estimate=pl.CostEstimate(
            flops=12 * rows * width * hidden,
            bytes_accessed=12 * width * hidden,
            transcendentals=2 * rows * hidden,
        ),
    )(x, row_weights, *own, *mate)


def in_three(values):
    parts = []
    for _ in range(3):
        part = lax.reduce_precision(values, 8, 7)
        parts.append(part.astype(jnp.bfloat16))
        values = values - part
    return jnp.concatenate(parts, axis=1)


def per_device(
    tokens,
    lengths,
    attn_gain,
    w_query,
    w_key,
    w_value,
    sinks,
    w_out,
    moe_gain,
    routes,
    route_weights,
    w_gate,
    w_up,
    w_down,
):
    tok_rows, model_width = tokens.shape
    devices = lax.axis_size("ctx")
    planes = devices // PLANE
    me = lax.axis_index("ctx")
    in_plane = me % PLANE
    half = lax.axis_index("groups") % 2
    info = jnp.stack([me, half]).astype(jnp.int32)
    cols = w_query.shape[1] // devices
    q_rows = w_query.shape[0]

    parts = split_query(info, w_query, planes)
    got = [parts[0]] + [swap_with(parts[m], "ctx", m) for m in (1, 2, 3)]
    odd = me % 2 == 1
    near_pair = jnp.concatenate(
        [jnp.where(odd, got[1], got[0]), jnp.where(odd, got[0], got[1])], axis=0
    )
    far_pair = jnp.concatenate(
        [jnp.where(odd, got[3], got[2]), jnp.where(odd, got[2], got[3])], axis=0
    )
    w_mine = jnp.where(half == 0, near_pair, far_pair)
    w_rest = jnp.where(half == 0, far_pair, near_pair)
    mine_of = over_planes(w_mine, planes)
    q_weights = [w_mine, w_rest]
    for k in range(1, planes):
        q_weights += [mine_of[k], swap_with(mine_of[k], "groups", 1)]
    w_across, w_beside, w_last = mine_of[planes // 2], mine_of[1], mine_of[planes - 1]

    own_slab = (w_gate, w_up, jnp.swapaxes(w_down, 1, 2))
    mate_slab = tuple(swap_with(after(w, got[1]), "ctx", 1) for w in own_slab)

    tokens = after(tokens, got[1])
    normed = rms_scale(tokens, attn_gain)
    wide_normed = jnp.pad(normed, ((0, 0), (0, lane_padded(model_width) - model_width)))
    y_normed = swap_with(after(wide_normed, got[2], got[3]), "ctx", 2)
    two = jnp.concatenate([wide_normed, after(y_normed, w_across, w_beside, *mate_slab)], axis=0)
    plane_tokens = jnp.concatenate([two, swap_with(two, "ctx", 1)], axis=0)
    nb = jnp.stack(
        [plane_tokens[:, 2 * b * q_rows:2 * (b + 1) * q_rows] for b in range(devices // 2)]
    )

    span = jnp.arange(tok_rows, dtype=jnp.int32)
    positions = jnp.concatenate([(me ^ m) * tok_rows + span for m in ORDER])
    cosine, sine = angle_tables(positions)
    raw_key = jnp.dot(normed, w_key, preferred_element_type=jnp.float32)
    val_flat = jnp.dot(normed, w_value, preferred_element_type=jnp.float32).astype(jnp.bfloat16)
    key_flat = rotate_key(raw_key, cosine[:tok_rows], sine[:tok_rows])
    facts = jnp.concatenate([routes.astype(jnp.bfloat16), in_three(route_weights)], axis=1)
    kv_width = key_flat.shape[1] + val_flat.shape[1]
    fact_width = facts.shape[1]
    facts = jnp.pad(facts, ((0, 0), (0, 128 - fact_width)))
    kv_of = over_planes(jnp.concatenate([key_flat, val_flat, facts], axis=1), planes)
    own_kv = jnp.concatenate([kv_of[k] for k in range(planes)], axis=0)
    y_kv = after(swap_with(own_kv, "ctx", 2), w_across, w_beside)
    c_kv = swap_with(jnp.concatenate([own_kv, y_kv], axis=0), "ctx", 1)

    short = w_out.shape[0] // 2
    wo_mine = jnp.where(half == 0, w_out[:short], w_out[short:])
    wo_of = over_planes(wo_mine, planes, (w_across, w_last))
    wo_parts = []
    for k in range(1, planes):
        wo_parts += [wo_of[k], swap_with(wo_of[k], "groups", 1)]

    experts_num = devices // SPLITS
    capacity = tok_rows * TOP * 17 // (16 * experts_num)
    padded = -(-capacity // 8) * 8

    def facts_of(block):
        return block[:, kv_width:kv_width + fact_width].reshape(planes, tok_rows, fact_width).astype(
            jnp.float32
        )

    own_facts, far_facts = facts_of(own_kv), facts_of(y_kv)
    mine_expert = (me // SPLITS).astype(jnp.float32)
    other_expert = ((me // SPLITS) ^ 1).astype(jnp.float32)
    earlier = (span[:, None] < span[None, :]).astype(jnp.bfloat16)
    slot_ids = jnp.arange(padded, dtype=jnp.float32)

    def chosen_rows(known, expert_id):
        match = known[:, :, :TOP] == expert_id
        hit = jnp.any(match, axis=2)
        weight = sum(known[:, :, i * TOP:(i + 1) * TOP] for i in (1, 2, 3))
        weight = jnp.sum(jnp.where(match, weight, 0.0), axis=2)
        slot = jnp.dot(hit.astype(jnp.bfloat16), earlier, preferred_element_type=jnp.float32)
        pick = hit[:, None, :] & (slot[:, None, :] == slot_ids[None, :, None])
        row_weight = jnp.sum(jnp.where(pick, weight[:, None, :], 0.0), axis=2)
        return pick.astype(jnp.bfloat16), row_weight

    pick_own, weight_own = chosen_rows(own_facts, mine_expert)
    pick_other, _ = chosen_rows(own_facts, other_expert)
    _, weight_far = chosen_rows(far_facts, mine_expert)
    pick_own, pick_other, weight_own, weight_far, info_late, _ = lax.optimization_barrier(
        (pick_own, pick_other, weight_own, weight_far, info, wo_of[planes // 2])
    )

    doc_ends = jnp.cumsum(lengths)
    lo = jnp.max(jnp.where(doc_ends[None, :] <= positions[:, None], doc_ends[None, :], 0), axis=1)
    heads_of = cols // HD
    my_sinks = lax.dynamic_index_in_dim(
        sinks.reshape(planes, PLANE, heads_of), in_plane, 1, keepdims=False
    ).reshape(-1)
    queries = make_queries(info_late, nb, cosine, sine, q_weights, planes, cols)
    attended = attend(
        after(info, wo_of[planes - 1]), lo[::tok_rows], my_sinks, queries, lo[:, None],
        positions[:, None], (own_kv, y_kv, c_kv), planes, cols,
    )
    send, keep = project(info, attended, w_out, wo_parts, planes)
    send, keep = add_core(keep, swap_with(send, "ctx", 1))
    mixed, expert_in = mix(tokens, keep, swap_with(send, "ctx", 2), moe_gain)

    def rows_for(pick, k, block):
        return jnp.dot(pick[k], block, preferred_element_type=jnp.float32).astype(jnp.bfloat16)

    def sent(k, block):
        rows = rows_for(pick_other, k, block)
        return rows, swap_with(rows, "ctx", 2)

    last = planes - 1
    near, far, ready = {}, {}, []
    first_rows, far[0] = sent(0, expert_in)
    blocks = over_planes(expert_in, planes, (mixed, first_rows))
    for k in range(planes - 1):
        near[k] = rows_for(pick_own, k, blocks[k])
        if k:
            rows, far[k] = sent(k, blocks[k])
            ready.append(rows)

    def run(parts):
        x = jnp.concatenate([rows for rows, _ in parts], axis=0)
        weights = jnp.concatenate([weight for _, weight in parts])
        out = expert(after(x, *ready), weights[:, None], own_slab, mate_slab)
        return [out[i * padded:(i + 1) * padded] for i in range(len(parts))]

    done, back = {}, {}
    first = run([(near[k], weight_own[k]) for k in range(last)] + [(far[0], weight_far[0])])
    for k in range(last):
        done[k] = first[k]
    back[0] = swap_with(first[last], "ctx", 2)
    block = after(blocks[last], first[0])
    _, far[last] = sent(last, block)
    near[last] = rows_for(pick_own, last, block)
    middle = list(range(1, last))
    second = run(
        [(near[last], weight_own[last]), (far[last], weight_far[last])]
        + [(far[k], weight_far[k]) for k in middle]
    )
    done[last] = second[0]
    back[last] = swap_with(second[1], "ctx", 2)
    late = after(jnp.concatenate(second[2:], axis=0), back[last])
    late = swap_with(late, "ctx", 2)
    for i, k in enumerate(middle):
        back[k] = late[i * padded:(i + 1) * padded]

    def gathered(pick, k, rows):
        return lax.dot_general(
            pick[k], rows, (((0,), (0,)), ((), ())), preferred_element_type=jnp.float32
        )

    sums = {k: gathered(pick_own, k, done[k]) + gathered(pick_other, k, back[k]) for k in done}
    ends = []
    bit = 1
    while bit < planes:
        for k in sorted(sums, reverse=True):
            if k & bit:
                arrived = swap_with(sums.pop(k).astype(jnp.bfloat16), "ctx", PLANE * bit)
                if k ^ bit:
                    sums[k ^ bit] = sums[k ^ bit] + arrived.astype(jnp.float32)
                else:
                    ends.append(arrived)
        bit *= 2
    return finish(mixed, sums[0], *ends)


def solution(mesh):
    placed = (
        P(("groups", "ctx"), None),
        P("groups"),
        P(),
        P("ctx", None),
        P(),
        P(),
        P(),
        P("ctx", None),
        P(),
        P(("groups", "ctx"), None),
        P(("groups", "ctx"), None),
        P("ctx", None, None),
        P("ctx", None, None),
        P("ctx", None, None),
    )
    return jax.shard_map(
        per_device,
        mesh=mesh,
        in_specs=placed,
        out_specs=P(("groups", "ctx"), None),
        check_vma=False,
    )
```

```python
import jax
import jax.numpy as jnp
import numpy as np
from jax import lax
from jax.experimental import pallas as pl
from jax.experimental.pallas import tpu as pltpu
from jax.sharding import PartitionSpec as P

HD = 64
SPLITS = 2
TOP = 4
PLANE = 4
ORDER = (0, 2, 1, 3)

EPS = 1e-05
THETA = 150000.0
ALPHA = 1.702
SCALE = 0.125
NEGATIVE = -1e30


def swap_with(x, axis, bits):
    return lax.ppermute(x, axis, [(i, i ^ bits) for i in range(lax.axis_size(axis))])


def after(value, *earlier):
    return lax.optimization_barrier((value, *earlier))[0]


def gate(value, *earlier):
    anywhere = pl.BlockSpec(memory_space=pl.ANY)
    return pl.pallas_call(
        lambda *refs: None,
        out_shape=jax.ShapeDtypeStruct(value.shape, value.dtype),
        in_specs=[anywhere] * (1 + len(earlier)),
        out_specs=anywhere,
        input_output_aliases={0: 0},
        compiler_params=pltpu.CompilerParams(vmem_limit_bytes=60 * 1024 * 1024),
    )(value, *earlier)


def forwarded(held, planes, hops):
    return {
        k: swap_with(held[k & (k - 1)], "ctx", PLANE * (k & -k))
        for k in range(planes - 1, 0, -1)
        if k.bit_count() == hops and k not in held
    }


def over_planes(block, planes):
    held = {0: block}
    for hops in range(1, planes.bit_length()):
        held.update(forwarded(held, planes, hops))
    return held


def together(*values):
    flat, tree = jax.tree.flatten(values)
    anywhere = pl.BlockSpec(memory_space=pl.ANY)
    out = pl.pallas_call(
        lambda *refs: None,
        out_shape=[jax.ShapeDtypeStruct(x.shape, x.dtype) for x in flat],
        in_specs=[anywhere] * len(flat),
        out_specs=[anywhere] * len(flat),
        input_output_aliases={i: i for i in range(len(flat))},
        compiler_params=pltpu.CompilerParams(vmem_limit_bytes=60 * 1024 * 1024),
    )(*flat)
    return jax.tree.unflatten(tree, out)


def lane_padded(width):
    return -(-width // 128) * 128


def rms_scale(values, gain_vec):
    wide = values.astype(jnp.float32)
    inverse = lax.rsqrt(jnp.mean(wide * wide, axis=-1, keepdims=True) + EPS)
    return (wide * inverse * gain_vec).astype(jnp.bfloat16)


def angle_tables(positions):
    half_size = HD // 2
    freqs = np.tile(THETA ** (-np.arange(half_size) / half_size), 4).astype(np.float32)
    sign = np.tile(np.repeat(np.array([-1.0, 1.0], np.float32), half_size), 2)
    angles = positions.astype(jnp.float32)[:, None] * freqs[None, :]
    return jnp.cos(angles), jnp.sin(angles) * sign[None, :]


def turn(tile, first, cosine, sine):
    width = 2 * HD
    other = jnp.where(first, pltpu.roll(tile, width - HD // 2, 1), pltpu.roll(tile, HD // 2, 1))
    return tile * cosine + other * sine


def whole_call(body, out_shapes, operands, scalars=1, scratch=(), limit=24, flops=0, waits=0):
    anywhere = pl.BlockSpec(memory_space=pl.ANY)
    smem = pl.BlockSpec(memory_space=pltpu.SMEM)
    vmem = pl.BlockSpec(memory_space=pltpu.VMEM)
    size = sum(x.size * x.dtype.itemsize for x in operands)
    return pl.pallas_call(
        body,
        out_shape=out_shapes,
        in_specs=[smem] * scalars + [vmem] * (len(operands) - scalars - waits) + [anywhere] * waits,
        out_specs=jax.tree.map(lambda _: vmem, out_shapes),
        scratch_shapes=list(scratch),
        compiler_params=pltpu.CompilerParams(vmem_limit_bytes=limit * 1024 * 1024),
        cost_estimate=pl.CostEstimate(flops=flops, bytes_accessed=size, transcendentals=0),
    )(*operands)


def split_query(info, w_query, planes):
    rows = w_query.shape[0]
    cols = w_query.shape[1] // (planes * PLANE)
    if cols % 128:
        in_plane = info[0] % PLANE
        parts = jnp.stack(
            [
                jnp.concatenate(
                    [
                        w_query[:, (PLANE * zz + j) * cols:(PLANE * zz + j + 1) * cols]
                        for zz in range(planes)
                    ],
                    axis=1,
                )
                for j in range(PLANE)
            ]
        )
        return [
            lax.dynamic_index_in_dim(parts, in_plane ^ m, 0, keepdims=False) for m in range(PLANE)
        ]

    def body(info_ref, w_ref, *outs):
        in_plane = info_ref[0] % PLANE
        for m in range(PLANE):
            for zz in range(planes):
                start = pl.multiple_of((PLANE * zz + (in_plane ^ m)) * cols, 128)
                outs[m][:, zz * cols:(zz + 1) * cols] = w_ref[:, pl.ds(start, cols)]

    shape = jax.ShapeDtypeStruct((rows, planes * cols), jnp.bfloat16)
    return whole_call(body, [shape] * PLANE, (info, w_query))


def prepare(tokens, gain, w_key, w_value, routes, route_weights, cosine, sine, earlier):
    rows, width = tokens.shape
    padded = lane_padded(width)
    key_cols = w_key.shape[1]

    def body(tok_ref, gain_ref, key_ref, val_ref, route_ref, weight_ref, cos_ref, sin_ref, _,
             rows_ref, normed_ref, kv_ref, wide):
        for start in range(0, width, 128):
            size = min(128, width - start)
            piece = tok_ref[start:start + size, :].astype(jnp.float32)
            if size < 128:
                piece = jnp.concatenate([piece, jnp.zeros((128 - size, rows), jnp.float32)], axis=0)
            wide[:, start:start + 128] = piece.T
        values = wide[...]
        rows_ref[...] = values.astype(jnp.bfloat16)
        mean = jnp.sum(values * values, axis=1, keepdims=True) / width
        normed_ref[...] = (values * lax.rsqrt(mean + EPS) * gain_ref[...]).astype(jnp.bfloat16)
        normed = normed_ref[:, :width]
        raw_key = jnp.dot(normed, key_ref[...], preferred_element_type=jnp.float32)
        lane = lax.broadcasted_iota(jnp.int32, (rows, 2 * HD), 1)
        first = lane % HD < HD // 2
        for start in range(0, key_cols, 2 * HD):
            lanes = slice(start, start + 2 * HD)
            kv_ref[:, lanes] = turn(raw_key[:, lanes], first, cos_ref[...], sin_ref[...]).astype(
                jnp.bfloat16
            )
        kv_ref[:, key_cols:2 * key_cols] = jnp.dot(
            normed, val_ref[...], preferred_element_type=jnp.float32
        ).astype(jnp.bfloat16)
        left = weight_ref[...]
        facts = [route_ref[...].astype(jnp.float32)]
        for _ in range(3):
            part = left.astype(jnp.bfloat16).astype(jnp.float32)
            facts.append(part)
            left = left - part
        facts.append(jnp.zeros((128 - 4 * TOP, rows), jnp.float32))
        kv_ref[:, 2 * key_cols:] = jnp.concatenate(facts, axis=0).T.astype(jnp.bfloat16)

    gain = jnp.pad(gain, (0, padded - width))[None]
    return whole_call(
        body,
        [
            jax.ShapeDtypeStruct((rows, padded), jnp.bfloat16),
            jax.ShapeDtypeStruct((rows, padded), jnp.bfloat16),
            jax.ShapeDtypeStruct((rows, 2 * key_cols + 128), jnp.bfloat16),
        ],
        (tokens.T, gain, w_key, w_value, routes.T, route_weights.T, cosine, sine, earlier),
        scalars=0,
        waits=1,
        scratch=[pltpu.VMEM((rows, padded), jnp.float32)],
        flops=1_000_000_000,
    )


def cut_pairs(two, c_two, pairs, cols):
    rows = two.shape[0]

    def body(two_ref, c_ref, out_ref):
        for b in range(pairs):
            lanes = slice(b * cols, (b + 1) * cols)
            out_ref[b, :rows, :] = two_ref[:, lanes]
            out_ref[b, rows:, :] = c_ref[:, lanes]

    return whole_call(
        body, jax.ShapeDtypeStruct((pairs, 2 * rows, cols), jnp.bfloat16), (two, c_two), scalars=0
    )


def joined(*blocks):
    rows = [block.shape[0] for block in blocks]

    def body(*refs):
        start = 0
        for ref, count in zip(refs[:-1], rows):
            refs[-1][start:start + count] = ref[...]
            start += count

    out = jax.ShapeDtypeStruct((sum(rows),) + blocks[0].shape[1:], blocks[0].dtype)
    return whole_call(body, out, blocks, scalars=0)


def half_rows(info, weight, earlier):
    rows, width = weight.shape
    padded = lane_padded(width)

    def body(info_ref, weight_ref, _, out_ref):
        at = pl.multiple_of(info_ref[1] * (rows // 2), rows // 2)
        out_ref[:, :width] = weight_ref[pl.ds(at, rows // 2), :]
        out_ref[:, width:] = jnp.zeros((rows // 2, padded - width), jnp.bfloat16)

    vmem = pl.BlockSpec(memory_space=pltpu.VMEM)
    return pl.pallas_call(
        body,
        out_shape=jax.ShapeDtypeStruct((rows // 2, padded), jnp.bfloat16),
        in_specs=[pl.BlockSpec(memory_space=pltpu.SMEM), vmem, pl.BlockSpec(memory_space=pl.ANY)],
        out_specs=vmem,
    )(info, weight, earlier)


def own_half(info, pieces, normed, earlier):
    rows, cols = pieces[0].shape

    def body(info_ref, p0, p1, p2, p3, normed_ref, *rest):
        mine_ref, rest_ref, again_ref = rest[-3:]
        odd = info_ref[0] % 2 == 1
        half = info_ref[1]
        again_ref[...] = normed_ref[...]
        for swapped in range(2):
            @pl.when(odd if swapped else jnp.logical_not(odd))
            def _():
                near = (p1, p0) if swapped else (p0, p1)
                far = (p3, p2) if swapped else (p2, p3)
                near = jnp.concatenate([near[0][...], near[1][...]], axis=0)
                far = jnp.concatenate([far[0][...], far[1][...]], axis=0)

                @pl.when(half == 0)
                def _():
                    mine_ref[...] = near
                    rest_ref[...] = far

                @pl.when(half == 1)
                def _():
                    mine_ref[...] = far
                    rest_ref[...] = near

    shape = jax.ShapeDtypeStruct((2 * rows, cols), jnp.bfloat16)
    again = jax.ShapeDtypeStruct(normed.shape, normed.dtype)
    return whole_call(
        body, [shape, shape, again], (info, *pieces, normed, *earlier), waits=len(earlier)
    )


def query_kernel(planes, kv_heads, rows_of, info, nb_ref, cos_ref, sin_ref, *rest):
    pieces = rest[: 2 * planes]
    q_ref, weights, sem = rest[2 * planes:]
    copies = [
        pltpu.make_async_copy(piece, weights.at[i], sem.at[i]) for i, piece in enumerate(pieces)
    ]
    for copy in copies:
        copy.start()
    me, half = info[0], info[1]
    width = 2 * HD
    wide = 2 * rows_of
    lane = lax.broadcasted_iota(jnp.int32, (wide, width), 1)
    low_half = lane < HD
    first = lane % HD < HD // 2
    for r in range(2):
        total = None
        for k in range(planes):
            for side in range(2):
                chosen = half if side == 0 else 1 - half
                pair = (me ^ (PLANE * k + 2 * chosen)) // 2
                if r == 0:
                    copies[2 * k + side].wait()
                term = jnp.dot(
                    nb_ref[pair, r * wide:(r + 1) * wide, :], weights[2 * k + side],
                    preferred_element_type=jnp.float32,
                )
                total = term if total is None else total + term
        at = slice(r * wide, (r + 1) * wide)
        for g in range(kv_heads):
            tile = total[:, g * width:(g + 1) * width]
            tile = turn(tile, first, cos_ref[at, :], sin_ref[at, :]) * SCALE
            moved = pltpu.roll(tile, HD, 1)
            if g % 2 == 0:
                heads = (jnp.where(low_half, tile, 0.0), jnp.where(low_half, moved, 0.0))
            else:
                heads = (jnp.where(low_half, 0.0, moved), jnp.where(low_half, 0.0, tile))
            for u in range(2):
                for m in range(2):
                    start = (2 * (2 * r + m) + u) * rows_of
                    q_ref[g, start:start + rows_of, :] = heads[u][
                        m * rows_of:(m + 1) * rows_of
                    ].astype(jnp.bfloat16)


def make_queries(info, nb, cosine, sine, weights, planes, cols):
    rows = cosine.shape[0]
    kv_heads = planes * cols // (2 * HD)

    def body(*refs):
        query_kernel(planes, kv_heads, rows // PLANE, *refs)

    smem = pl.BlockSpec(memory_space=pltpu.SMEM)
    vmem = pl.BlockSpec(memory_space=pltpu.VMEM)
    anywhere = pl.BlockSpec(memory_space=pl.ANY)
    return pl.pallas_call(
        body,
        out_shape=jax.ShapeDtypeStruct((kv_heads, 2 * rows, 2 * HD), jnp.bfloat16),
        in_specs=[smem] + [vmem] * 3 + [anywhere] * len(weights),
        out_specs=vmem,
        scratch_shapes=[
            pltpu.VMEM((len(weights),) + weights[0].shape, jnp.bfloat16),
            pltpu.SemaphoreType.DMA((len(weights),)),
        ],
        compiler_params=pltpu.CompilerParams(vmem_limit_bytes=56 * 1024 * 1024),
        cost_estimate=pl.CostEstimate(
            flops=8_000_000_000, bytes_accessed=8_000_000, transcendentals=0
        ),
    )(info, nb, cosine, sine, *weights)


def attention_kernel(planes, kv_heads, rows_of, info, lo_first, sink_ref, q_ref, lo_ref, pos_ref,
                     own_kv, y_kv, c_kv, cy_kv, out_ref, bias_ref, score_ref, max_ref, acc_ref):
    me = info[0]
    plane = me // PLANE
    rows = PLANE * rows_of
    width = 2 * HD
    wide = 2 * rows_of
    cols = out_ref.shape[2]
    earliest = lo_first[0]
    for m in range(1, PLANE):
        earliest = jnp.minimum(earliest, lo_first[m])

    def for_needed(act):
        def step(k, carry):
            other = plane ^ k

            @pl.when((other <= plane) & (earliest < (other + 1) * rows))
            def _():
                act(k)

            return carry

        lax.fori_loop(0, planes, step, 0)

    def chunk(k, lanes):
        at = pl.ds(pl.multiple_of(k * rows_of, rows_of), rows_of)
        return jnp.concatenate(
            [own_kv[at, lanes], y_kv[at, lanes], c_kv[at, lanes], cy_kv[at, lanes]], axis=0
        )

    key_iota = lax.broadcasted_iota(jnp.int32, (1, rows_of), 1)

    def set_bias(k):
        key_pos = jnp.concatenate(
            [(me ^ (PLANE * k + m)) * rows_of + key_iota for m in ORDER], axis=1
        )
        allowed = (key_pos >= lo_ref[...]) & (key_pos <= pos_ref[...])
        bias_ref[k] = jnp.where(allowed, 0.0, NEGATIVE)

    for_needed(set_bias)

    lane_q = lax.broadcasted_iota(jnp.int32, (wide, width), 1) < HD
    lane_k = lax.broadcasted_iota(jnp.int32, (rows, width), 1) < HD
    row_q = lax.broadcasted_iota(jnp.int32, (wide, width), 0) < rows_of

    def two_heads(pair, carry):
        key_lanes = pl.ds(pl.multiple_of(pair * width, width), width)
        val_lanes = pl.ds(pl.multiple_of((kv_heads // 2 + pair) * width, width), width)
        sinks = [
            jnp.where(row_q, sink_ref[4 * pair + 2 * i], sink_ref[4 * pair + 2 * i + 1])
            for i in range(2)
        ]
        for i in range(2):
            for m in range(PLANE):
                max_ref[i, m * wide:(m + 1) * wide, :] = sinks[i]

        def scores(k):
            keys = chunk(k, key_lanes)
            for m in range(PLANE):
                at = slice(m * wide, (m + 1) * wide)
                bias = bias_ref[k, m * rows_of:(m + 1) * rows_of, :]
                for i in range(2):
                    score = lax.dot_general(
                        q_ref[2 * pair + i, at, :], keys, (((1,), (1,)), ((), ())),
                        preferred_element_type=jnp.float32,
                    )
                    score = (score.reshape(2, rows_of, rows) + bias[None]).reshape(wide, rows)
                    score_ref[i, k, at, :] = score
                    top = max_ref[i, at, :]
                    for start in range(0, rows, width):
                        top = jnp.maximum(top, score[:, start:start + width])
                    max_ref[i, at, :] = top

        for_needed(scores)

        for i in range(2):
            mine = lane_q if i == 0 else ~lane_q
            for m in range(PLANE):
                at = slice(m * wide, (m + 1) * wide)
                top = jnp.max(max_ref[i, at, :], axis=1, keepdims=True)
                top = jnp.broadcast_to(top, (wide, width))
                max_ref[i, at, :] = top
                acc_ref[i, at, :] = jnp.where(mine, 0.0, jnp.exp(sinks[i] - top))

        def gather(k):
            values = chunk(k, val_lanes)
            for i in range(2):
                mine_k = lane_k if i == 0 else ~lane_k
                vals = jnp.where(mine_k, values, jnp.bfloat16(1.0))
                for m in range(PLANE):
                    at = slice(m * wide, (m + 1) * wide)
                    top = max_ref[i, at, :]
                    probs = jnp.concatenate(
                        [
                            jnp.exp(score_ref[i, k, at, start:start + width] - top).astype(
                                jnp.bfloat16
                            )
                            for start in range(0, rows, width)
                        ],
                        axis=1,
                    )
                    acc_ref[i, at, :] += jnp.dot(probs, vals, preferred_element_type=jnp.float32)

        for_needed(gather)

        for i in range(2):
            g = 2 * pair + i
            for m in range(PLANE):
                acc = acc_ref[i, m * wide:(m + 1) * wide, :]
                done = acc / pltpu.roll(acc, HD, 1)
                one, two = done[:rows_of], done[rows_of:]
                low = lane_q[:rows_of]
                if i == 0:
                    both = jnp.where(low, one, pltpu.roll(two, HD, 1))
                else:
                    both = jnp.where(low, pltpu.roll(one, HD, 1), two)
                both = both.astype(jnp.bfloat16)
                for j in range(width // cols):
                    out_ref[g * (width // cols) + j, m * rows_of:(m + 1) * rows_of, :] = both[
                        :, j * cols:(j + 1) * cols
                    ]
        return carry

    lax.fori_loop(0, kv_heads // 2, two_heads, 0)


def attend(info, lo_first, sinks, queries, lo, pos, kv, planes, cols):
    rows = pos.shape[0]
    kv_heads = queries.shape[0]

    def body(*refs):
        attention_kernel(planes, kv_heads, rows // PLANE, *refs)

    return whole_call(
        body,
        jax.ShapeDtypeStruct((planes, rows, cols), jnp.bfloat16),
        (info, lo_first, sinks, queries, lo, pos, *kv),
        scalars=3,
        scratch=[
            pltpu.VMEM((planes, rows, rows), jnp.float32),
            pltpu.VMEM((2, planes, 2 * rows, rows), jnp.float32),
            pltpu.VMEM((2, 2 * rows, 2 * HD), jnp.float32),
            pltpu.VMEM((2, 2 * rows, 2 * HD), jnp.float32),
        ],
        limit=58,
        flops=16_000_000_000,
    )


def project(info, attended, own, mine, twin, places):
    planes, rows, cols = attended.shape
    width = own.shape[1]
    padded = lane_padded(width)
    wide = rows // 2

    def body(info_ref, att_ref, own_ref, *rest):
        send_ref, keep_ref, att, weight = rest[2 * len(places):]
        plane, half = info_ref[0] // PLANE, info_ref[1]
        short = cols // 2
        weight[:cols, :] = own_ref[...]
        for k in range(planes):
            att[:, k * cols:(k + 1) * cols] = att_ref[plane ^ k]
        for i, ks in enumerate(places):
            for side in range(2):
                chosen = half if side == 0 else 1 - half
                for j, k in enumerate(ks):
                    at = pl.multiple_of(k * cols + chosen * short, short)
                    weight[pl.ds(at, short), :] = rest[side * len(places) + i][
                        j * short:(j + 1) * short, :width
                    ]
        for start in range(0, width, 640):
            lanes = slice(start, min(width, start + 640))
            send_ref[:, lanes] = jnp.dot(
                att[wide:], weight[:, lanes], preferred_element_type=jnp.float32
            ).astype(jnp.bfloat16)
            keep_ref[:, lanes] = jnp.dot(
                att[:wide], weight[:, lanes], preferred_element_type=jnp.float32
            )
        send_ref[:, width:] = jnp.zeros((wide, padded - width), jnp.bfloat16)
        keep_ref[:, width:] = jnp.zeros((wide, padded - width), jnp.float32)

    return whole_call(
        body,
        [
            jax.ShapeDtypeStruct((wide, padded), jnp.bfloat16),
            jax.ShapeDtypeStruct((wide, padded), jnp.float32),
        ],
        (info, attended, own, *mine, *twin),
        scratch=[
            pltpu.VMEM((rows, planes * cols), jnp.bfloat16),
            pltpu.VMEM((planes * cols, width), jnp.bfloat16),
        ],
        flops=4_000_000_000,
    )


def add_core(keep, got):
    rows, width = keep.shape[0] // 2, keep.shape[1]

    def body(keep_ref, got_ref, send_ref, rest_ref):
        rest_ref[...] = keep_ref[:rows] + got_ref[:rows].astype(jnp.float32)
        send_ref[...] = (keep_ref[rows:] + got_ref[rows:].astype(jnp.float32)).astype(jnp.bfloat16)

    return whole_call(
        body,
        [
            jax.ShapeDtypeStruct((rows, width), jnp.bfloat16),
            jax.ShapeDtypeStruct((rows, width), jnp.float32),
        ],
        (keep, got),
        scalars=0,
    )


def mix(tokens, keep, got, gain):
    rows, padded = tokens.shape
    width = gain.shape[0]

    def body(tokens_ref, keep_ref, got_ref, gain_ref, mixed_ref, in_ref):
        mixed = (
            tokens_ref[...].astype(jnp.float32) + keep_ref[...] + got_ref[...].astype(jnp.float32)
        ).astype(jnp.bfloat16)
        mixed_ref[...] = mixed
        values = mixed.astype(jnp.float32)
        mean = jnp.sum(values * values, axis=1, keepdims=True) / width
        in_ref[...] = (values * lax.rsqrt(mean + EPS) * gain_ref[...]).astype(jnp.bfloat16)

    shape = jax.ShapeDtypeStruct((rows, padded), jnp.bfloat16)
    gain = jnp.pad(gain, (0, padded - width))[None]
    return whole_call(body, [shape, shape], (tokens, keep, got, gain), scalars=0)


def finish(width, mixed, total, *got):
    rows = mixed.shape[0]

    def body(mixed_ref, total_ref, *rest):
        out_ref = rest[-1]
        for start in range(0, width, 128):
            size = min(128, width - start)
            lanes = slice(start, start + size)
            value = mixed_ref[:, lanes].astype(jnp.float32) + total_ref[:, lanes]
            for ref in rest[:-1]:
                value += ref[:, lanes].astype(jnp.float32)
            if size < 128:
                value = jnp.concatenate([value, jnp.zeros((rows, 128 - size), jnp.float32)], axis=1)
            out_ref[lanes, :] = value.T[:size].astype(jnp.bfloat16)

    out = jax.ShapeDtypeStruct((width, rows), jnp.bfloat16)
    return whole_call(body, out, (mixed, total, *got), scalars=0).T


def by_columns(hidden, down):
    return lax.dot_general(hidden, down, (((1,), (1,)), ((), ())), preferred_element_type=jnp.float32)


def expert(x, row_weights, slabs):
    rows, padded = x.shape
    width, hidden = slabs[0].shape[1:]

    def body(x_ref, row_ref, gate_ref, up_ref, down_ref, out_ref, held, sem):
        copies = [
            pltpu.make_async_copy(ref.at[side], held.at[3 * side + i], sem.at[3 * side + i])
            for side in range(2)
            for i, ref in enumerate((gate_ref, up_ref, down_ref))
        ]
        for copy in copies[:2]:
            copy.start()
        total = None
        for side in range(2):
            i = 3 * side
            inputs = x_ref[:, :width]
            copies[i].wait()
            copies[i + 2].start()
            gate_val = jnp.dot(inputs, held[i], preferred_element_type=jnp.float32)
            copies[i + 1].wait()
            if side == 0:
                copies[3].start()
                copies[4].start()
            up_val = jnp.dot(inputs, held[i + 1], preferred_element_type=jnp.float32)
            rows_in = ((up_val + 1.0) * gate_val * jax.nn.sigmoid(ALPHA * gate_val)).astype(
                jnp.bfloat16
            )
            copies[i + 2].wait()
            term = by_columns(rows_in, held[i + 2])
            total = term if total is None else total + term
        out_ref[:, :width] = (total * row_ref[...]).astype(jnp.bfloat16)
        out_ref[:, width:] = jnp.zeros((rows, padded - width), jnp.bfloat16)

    vmem = pl.BlockSpec(memory_space=pltpu.VMEM)
    return pl.pallas_call(
        body,
        out_shape=jax.ShapeDtypeStruct((rows, padded), jnp.bfloat16),
        in_specs=[vmem, vmem] + [pl.BlockSpec(memory_space=pl.ANY)] * 3,
        out_specs=vmem,
        scratch_shapes=[
            pltpu.VMEM((6, width, hidden), jnp.bfloat16),
            pltpu.SemaphoreType.DMA((6,)),
        ],
        compiler_params=pltpu.CompilerParams(vmem_limit_bytes=48 * 1024 * 1024),
        cost_estimate=pl.CostEstimate(
            flops=12 * rows * width * hidden,
            bytes_accessed=12 * width * hidden,
            transcendentals=2 * rows * hidden,
        ),
    )(x, row_weights, *slabs)


def per_device(
    tokens,
    lengths,
    attn_gain,
    w_query,
    w_key,
    w_value,
    sinks,
    w_out,
    moe_gain,
    routes,
    route_weights,
    w_gate,
    w_up,
    w_down,
):
    tok_rows, model_width = tokens.shape
    devices = lax.axis_size("ctx")
    planes = devices // PLANE
    me = lax.axis_index("ctx")
    in_plane = me % PLANE
    half = lax.axis_index("groups") % 2
    info = jnp.stack([me, half]).astype(jnp.int32)
    cols = w_query.shape[1] // devices
    q_rows = w_query.shape[0]

    cores = [[i, i + 1] for i in range(0, devices, 2)]
    slabs = [
        lax.all_gather(w, "ctx", axis=0, tiled=True, axis_index_groups=cores)
        for w in (w_gate, w_up, jnp.swapaxes(w_down, 1, 2))
    ]

    parts = split_query(info, w_query, planes)
    got = [swap_with(parts[m], "ctx", m) for m in (1, 2, 3)]

    span = jnp.arange(tok_rows, dtype=jnp.int32)
    positions = jnp.concatenate([(me ^ m) * tok_rows + span for m in ORDER])
    cosine, sine = angle_tables(positions)
    tokens, normed, kv = prepare(
        tokens, attn_gain, w_key, w_value, routes, route_weights, cosine[:tok_rows], sine[:tok_rows],
        parts[1],
    )
    kv_width, fact_width = w_key.shape[1] + w_value.shape[1], 4 * TOP

    w_mine, w_rest, late_normed = own_half(info, [parts[0], *got], normed, [])
    w_of = {0: w_mine}
    w_of.update(forwarded(w_of, planes, 1))
    kv_of = {0: kv}
    kv_of.update(forwarded(kv_of, planes, 1))
    y_normed = swap_with(late_normed, "ctx", 2)
    w_of, kv_of, y_normed = together(w_of, kv_of, y_normed)

    w_twin = {k: swap_with(w_of[k], "groups", 1) for k in w_of if k}
    w_of.update(forwarded(w_of, planes, 2))
    for hops in range(2, planes.bit_length()):
        kv_of.update(forwarded(kv_of, planes, hops))
    across = planes // 2
    wo_half = half_rows(info, w_out, y_normed)
    wo_of = {across: swap_with(wo_half, "ctx", PLANE * across)}
    w_of, w_twin, kv_of, y_normed, wo_half, wo_of = together(
        w_of, w_twin, kv_of, y_normed, wo_half, wo_of
    )

    for hops in range(3, planes.bit_length()):
        w_of.update(forwarded(w_of, planes, hops))
    two = joined(normed, y_normed)
    nb = cut_pairs(two, swap_with(two, "ctx", 1), devices // 2, 2 * q_rows)
    for k in w_of:
        if k and k not in w_twin:
            w_of[k] = gate(w_of[k], nb)
            w_twin[k] = swap_with(w_of[k], "groups", 1)
    own_kv = joined(*[kv_of[k] for k in range(planes)])
    y_kv = swap_with(own_kv, "ctx", 2)
    wo_twin = [swap_with(wo_of[across], "groups", 1)]
    wo_got, wo_ks, known = [wo_of[across]], [[across]], [0, across]
    bit = across // 2
    while bit:
        wo_got.append(swap_with(joined(wo_half, *wo_got), "ctx", PLANE * bit))
        wo_ks.append([k ^ bit for k in known])
        known += wo_ks[-1]
        bit //= 2
    w_twin, own_kv, y_kv, wo_got, wo_twin = together(w_twin, own_kv, y_kv, wo_got, wo_twin)

    c_kv = swap_with(own_kv, "ctx", 1)
    cy_kv = swap_with(y_kv, "ctx", 1)
    q_weights = [w_of[0], w_rest]
    for k in range(1, planes):
        q_weights += [w_of[k], w_twin[k]]
    wo_twin += [swap_with(rows, "groups", 1) for rows in wo_got[1:]]

    experts_num = devices // SPLITS
    capacity = tok_rows * TOP * 17 // (16 * experts_num)
    padded = -(-capacity // 8) * 8

    def facts_of(block):
        return block[:, kv_width:kv_width + fact_width].reshape(planes, tok_rows, fact_width).astype(
            jnp.float32
        )

    own_facts, far_facts = facts_of(own_kv), facts_of(y_kv)
    mine_expert = (me // SPLITS).astype(jnp.float32)
    other_expert = ((me // SPLITS) ^ 1).astype(jnp.float32)
    earlier = (span[:, None] < span[None, :]).astype(jnp.bfloat16)
    slot_ids = jnp.arange(padded, dtype=jnp.float32)

    def chosen_rows(known, expert_id):
        match = known[:, :, :TOP] == expert_id
        hit = jnp.any(match, axis=2)
        weight = sum(known[:, :, i * TOP:(i + 1) * TOP] for i in (1, 2, 3))
        weight = jnp.sum(jnp.where(match, weight, 0.0), axis=2)
        slot = jnp.dot(hit.astype(jnp.bfloat16), earlier, preferred_element_type=jnp.float32)
        pick = hit[:, None, :] & (slot[:, None, :] == slot_ids[None, :, None])
        row_weight = jnp.sum(jnp.where(pick, weight[:, None, :], 0.0), axis=2)
        return pick.astype(jnp.bfloat16), row_weight

    pick_own, weight_own = chosen_rows(own_facts, mine_expert)
    pick_other, _ = chosen_rows(own_facts, other_expert)
    _, weight_far = chosen_rows(far_facts, mine_expert)
    doc_ends = jnp.cumsum(lengths)
    lo = jnp.max(jnp.where(doc_ends[None, :] <= positions[:, None], doc_ends[None, :], 0), axis=1)
    heads_of = cols // HD
    my_sinks = lax.dynamic_index_in_dim(
        sinks.reshape(planes, PLANE, heads_of), in_plane, 1, keepdims=False
    ).reshape(-1)
    queries = make_queries(info, nb, cosine, sine, q_weights, planes, cols)
    attended = attend(
        info, lo[::tok_rows], my_sinks, queries, lo[:, None], positions[:, None],
        (own_kv, y_kv, c_kv, cy_kv), planes, cols,
    )
    send, keep = project(info, attended, w_out, wo_got, wo_twin, wo_ks)
    send, keep = add_core(keep, swap_with(send, "ctx", 1))
    mixed, expert_in = mix(tokens, keep, swap_with(send, "ctx", 2), moe_gain)

    def rows_for(pick, k, block):
        return jnp.dot(pick[k], block, preferred_element_type=jnp.float32).astype(jnp.bfloat16)

    def sent(k, block):
        rows = rows_for(pick_other, k, block)
        return rows, swap_with(rows, "ctx", 2)

    last = planes - 1
    near, far, ready = {}, {}, []
    first_rows, far[0] = sent(0, expert_in)
    blocks = over_planes(expert_in, planes)
    for k in range(planes - 1):
        near[k] = rows_for(pick_own, k, blocks[k])
        if k:
            rows, far[k] = sent(k, blocks[k])
            ready.append(rows)

    def run(parts):
        x = jnp.concatenate([rows for rows, _ in parts], axis=0)
        weights = jnp.concatenate([weight for _, weight in parts])
        out = expert(after(x, *ready), weights[:, None], slabs)
        return [out[i * padded:(i + 1) * padded] for i in range(len(parts))]

    done, back = {}, {}
    first = run([(near[k], weight_own[k]) for k in range(last)] + [(far[0], weight_far[0])])
    for k in range(last):
        done[k] = first[k]
    back[0] = swap_with(first[last], "ctx", 2)
    block = after(blocks[last], first[0])
    _, far[last] = sent(last, block)
    near[last] = rows_for(pick_own, last, block)
    middle = list(range(1, last))
    second = run(
        [(near[last], weight_own[last]), (far[last], weight_far[last])]
        + [(far[k], weight_far[k]) for k in middle]
    )
    done[last] = second[0]
    back[last] = swap_with(second[1], "ctx", 2)
    late = after(jnp.concatenate(second[2:], axis=0), back[last])
    late = swap_with(late, "ctx", 2)
    for i, k in enumerate(middle):
        back[k] = late[i * padded:(i + 1) * padded]

    def gathered(pick, k, rows):
        return lax.dot_general(
            pick[k], rows, (((0,), (0,)), ((), ())), preferred_element_type=jnp.float32
        )

    sums = {k: gathered(pick_own, k, done[k]) + gathered(pick_other, k, back[k]) for k in done}
    ends = []
    bit = 1
    while bit < planes:
        for k in sorted(sums, reverse=True):
            if k & bit:
                arrived = swap_with(sums.pop(k).astype(jnp.bfloat16), "ctx", PLANE * bit)
                if k ^ bit:
                    sums[k ^ bit] = sums[k ^ bit] + arrived.astype(jnp.float32)
                else:
                    ends.append(arrived)
        bit *= 2
    return finish(model_width, mixed, sums[0], *ends)


def solution(mesh):
    placed = (
        P(("groups", "ctx"), None),
        P("groups"),
        P(),
        P("ctx", None),
        P(),
        P(),
        P(),
        P("ctx", None),
        P(),
        P(("groups", "ctx"), None),
        P(("groups", "ctx"), None),
        P("ctx", None, None),
        P("ctx", None, None),
        P("ctx", None, None),
    )
    return jax.shard_map(
        per_device,
        mesh=mesh,
        in_specs=placed,
        out_specs=P(("groups", "ctx"), None),
        check_vma=False,
    )
```

```python
import jax
import jax.numpy as jnp
import numpy as np
from jax import lax
from jax.experimental import pallas as pl
from jax.experimental.pallas import tpu as pltpu
from jax.sharding import PartitionSpec as P

HD = 64
SPLITS = 2
TOP = 4
PLANE = 4
ORDER = (0, 2, 1, 3)

EPS = 1e-05
THETA = 150000.0
ALPHA = 1.702
SCALE = 0.125
NEGATIVE = -1e30


def swap_with(x, axis, bits):
    return lax.ppermute(x, axis, [(i, i ^ bits) for i in range(lax.axis_size(axis))])


def after(value, *earlier):
    return lax.optimization_barrier((value, *earlier))[0]


def gate(value, *earlier):
    anywhere = pl.BlockSpec(memory_space=pl.ANY)
    return pl.pallas_call(
        lambda *refs: None,
        out_shape=jax.ShapeDtypeStruct(value.shape, value.dtype),
        in_specs=[anywhere] * (1 + len(earlier)),
        out_specs=anywhere,
        input_output_aliases={0: 0},
    )(value, *earlier)


def forwarded(held, planes, hops):
    return {
        k: swap_with(held[k & (k - 1)], "ctx", PLANE * (k & -k))
        for k in range(planes - 1, 0, -1)
        if k.bit_count() == hops and k not in held
    }


def over_planes(block, planes):
    held = {0: block}
    for hops in range(1, planes.bit_length()):
        held.update(forwarded(held, planes, hops))
    return held


def together(*values):
    flat, tree = jax.tree.flatten(values)
    anywhere = pl.BlockSpec(memory_space=pl.ANY)
    out = pl.pallas_call(
        lambda *refs: None,
        out_shape=[jax.ShapeDtypeStruct(x.shape, x.dtype) for x in flat],
        in_specs=[anywhere] * len(flat),
        out_specs=[anywhere] * len(flat),
        input_output_aliases={i: i for i in range(len(flat))},
        compiler_params=pltpu.CompilerParams(vmem_limit_bytes=60 * 1024 * 1024),
    )(*flat)
    return jax.tree.unflatten(tree, out)


def lane_padded(width):
    return -(-width // 128) * 128


def rms_scale(values, gain_vec):
    wide = values.astype(jnp.float32)
    inverse = lax.rsqrt(jnp.mean(wide * wide, axis=-1, keepdims=True) + EPS)
    return (wide * inverse * gain_vec).astype(jnp.bfloat16)


def angle_tables(positions):
    half_size = HD // 2
    freqs = np.tile(THETA ** (-np.arange(half_size) / half_size), 4).astype(np.float32)
    sign = np.tile(np.repeat(np.array([-1.0, 1.0], np.float32), half_size), 2)
    angles = positions.astype(jnp.float32)[:, None] * freqs[None, :]
    return jnp.cos(angles), jnp.sin(angles) * sign[None, :]


def turn(tile, first, cosine, sine):
    width = 2 * HD
    other = jnp.where(first, pltpu.roll(tile, width - HD // 2, 1), pltpu.roll(tile, HD // 2, 1))
    return tile * cosine + other * sine


def whole_call(body, out_shapes, operands, scalars=1, scratch=(), limit=24, flops=0, waits=0):
    anywhere = pl.BlockSpec(memory_space=pl.ANY)
    smem = pl.BlockSpec(memory_space=pltpu.SMEM)
    vmem = pl.BlockSpec(memory_space=pltpu.VMEM)
    size = sum(x.size * x.dtype.itemsize for x in operands)
    return pl.pallas_call(
        body,
        out_shape=out_shapes,
        in_specs=[smem] * scalars + [vmem] * (len(operands) - scalars - waits) + [anywhere] * waits,
        out_specs=jax.tree.map(lambda _: vmem, out_shapes),
        scratch_shapes=list(scratch),
        compiler_params=pltpu.CompilerParams(vmem_limit_bytes=limit * 1024 * 1024),
        cost_estimate=pl.CostEstimate(flops=flops, bytes_accessed=size, transcendentals=0),
    )(*operands)


def split_query(info, w_query, planes):
    rows = w_query.shape[0]
    cols = w_query.shape[1] // (planes * PLANE)
    if cols % 128:
        in_plane = info[0] % PLANE
        parts = jnp.stack(
            [
                jnp.concatenate(
                    [
                        w_query[:, (PLANE * zz + j) * cols:(PLANE * zz + j + 1) * cols]
                        for zz in range(planes)
                    ],
                    axis=1,
                )
                for j in range(PLANE)
            ]
        )
        return [
            lax.dynamic_index_in_dim(parts, in_plane ^ m, 0, keepdims=False) for m in range(PLANE)
        ]

    def body(info_ref, w_ref, *outs):
        in_plane = info_ref[0] % PLANE
        for m in range(PLANE):
            for zz in range(planes):
                start = pl.multiple_of((PLANE * zz + (in_plane ^ m)) * cols, 128)
                outs[m][:, zz * cols:(zz + 1) * cols] = w_ref[:, pl.ds(start, cols)]

    shape = jax.ShapeDtypeStruct((rows, planes * cols), jnp.bfloat16)
    return whole_call(body, [shape] * PLANE, (info, w_query))


def prepare(tokens, gain, w_key, w_value, routes, route_weights, cosine, sine, earlier):
    rows, width = tokens.shape
    padded = lane_padded(width)
    key_cols = w_key.shape[1]

    def body(tok_ref, gain_ref, key_ref, val_ref, route_ref, weight_ref, cos_ref, sin_ref, _,
             rows_ref, normed_ref, kv_ref, wide):
        for start in range(0, width, 128):
            size = min(128, width - start)
            piece = tok_ref[start:start + size, :].astype(jnp.float32)
            if size < 128:
                piece = jnp.concatenate([piece, jnp.zeros((128 - size, rows), jnp.float32)], axis=0)
            wide[:, start:start + 128] = piece.T
        values = wide[...]
        rows_ref[...] = values.astype(jnp.bfloat16)
        mean = jnp.sum(values * values, axis=1, keepdims=True) / width
        normed_ref[...] = (values * lax.rsqrt(mean + EPS) * gain_ref[...]).astype(jnp.bfloat16)
        normed = normed_ref[:, :width]
        raw_key = jnp.dot(normed, key_ref[...], preferred_element_type=jnp.float32)
        lane = lax.broadcasted_iota(jnp.int32, (rows, 2 * HD), 1)
        first = lane % HD < HD // 2
        for start in range(0, key_cols, 2 * HD):
            lanes = slice(start, start + 2 * HD)
            kv_ref[:, lanes] = turn(raw_key[:, lanes], first, cos_ref[...], sin_ref[...]).astype(
                jnp.bfloat16
            )
        kv_ref[:, key_cols:2 * key_cols] = jnp.dot(
            normed, val_ref[...], preferred_element_type=jnp.float32
        ).astype(jnp.bfloat16)
        left = weight_ref[...]
        facts = [route_ref[...].astype(jnp.float32)]
        for _ in range(3):
            part = left.astype(jnp.bfloat16).astype(jnp.float32)
            facts.append(part)
            left = left - part
        facts.append(jnp.zeros((128 - 4 * TOP, rows), jnp.float32))
        kv_ref[:, 2 * key_cols:] = jnp.concatenate(facts, axis=0).T.astype(jnp.bfloat16)

    gain = jnp.pad(gain, (0, padded - width))[None]
    return whole_call(
        body,
        [
            jax.ShapeDtypeStruct((rows, padded), jnp.bfloat16),
            jax.ShapeDtypeStruct((rows, padded), jnp.bfloat16),
            jax.ShapeDtypeStruct((rows, 2 * key_cols + 128), jnp.bfloat16),
        ],
        (tokens.T, gain, w_key, w_value, routes.T, route_weights.T, cosine, sine, earlier),
        scalars=0,
        waits=1,
        scratch=[pltpu.VMEM((rows, padded), jnp.float32)],
        flops=1_000_000_000,
    )


def cut_pairs(two, c_two, pairs, cols):
    rows = two.shape[0]

    def body(two_ref, c_ref, out_ref):
        for b in range(pairs):
            lanes = slice(b * cols, (b + 1) * cols)
            out_ref[b, :rows, :] = two_ref[:, lanes]
            out_ref[b, rows:, :] = c_ref[:, lanes]

    return whole_call(
        body, jax.ShapeDtypeStruct((pairs, 2 * rows, cols), jnp.bfloat16), (two, c_two), scalars=0
    )


def joined(*blocks):
    rows = [block.shape[0] for block in blocks]

    def body(*refs):
        start = 0
        for ref, count in zip(refs[:-1], rows):
            refs[-1][start:start + count] = ref[...]
            start += count

    out = jax.ShapeDtypeStruct((sum(rows),) + blocks[0].shape[1:], blocks[0].dtype)
    return whole_call(body, out, blocks, scalars=0)


def half_rows(info, weight, earlier):
    rows, width = weight.shape
    padded = lane_padded(width)

    def body(info_ref, weight_ref, _, out_ref):
        at = pl.multiple_of(info_ref[1] * (rows // 2), rows // 2)
        out_ref[:, :width] = weight_ref[pl.ds(at, rows // 2), :]
        out_ref[:, width:] = jnp.zeros((rows // 2, padded - width), jnp.bfloat16)

    vmem = pl.BlockSpec(memory_space=pltpu.VMEM)
    return pl.pallas_call(
        body,
        out_shape=jax.ShapeDtypeStruct((rows // 2, padded), jnp.bfloat16),
        in_specs=[pl.BlockSpec(memory_space=pltpu.SMEM), vmem, pl.BlockSpec(memory_space=pl.ANY)],
        out_specs=vmem,
    )(info, weight, earlier)


def own_half(info, pieces, normed, earlier):
    rows, cols = pieces[0].shape

    def body(info_ref, p0, p1, p2, p3, normed_ref, *rest):
        mine_ref, rest_ref, again_ref = rest[-3:]
        odd = info_ref[0] % 2 == 1
        half = info_ref[1]
        again_ref[...] = normed_ref[...]
        for swapped in range(2):
            @pl.when(odd if swapped else jnp.logical_not(odd))
            def _():
                near = (p1, p0) if swapped else (p0, p1)
                far = (p3, p2) if swapped else (p2, p3)
                near = jnp.concatenate([near[0][...], near[1][...]], axis=0)
                far = jnp.concatenate([far[0][...], far[1][...]], axis=0)

                @pl.when(half == 0)
                def _():
                    mine_ref[...] = near
                    rest_ref[...] = far

                @pl.when(half == 1)
                def _():
                    mine_ref[...] = far
                    rest_ref[...] = near

    shape = jax.ShapeDtypeStruct((2 * rows, cols), jnp.bfloat16)
    again = jax.ShapeDtypeStruct(normed.shape, normed.dtype)
    return whole_call(
        body, [shape, shape, again], (info, *pieces, normed, *earlier), waits=len(earlier)
    )


def query_kernel(planes, kv_heads, rows_of, info, nb_ref, cos_ref, sin_ref, *rest):
    pieces = rest[: 2 * planes]
    q_ref, weights, sem = rest[2 * planes:]
    copies = [
        pltpu.make_async_copy(piece, weights.at[i], sem.at[i]) for i, piece in enumerate(pieces)
    ]
    for copy in copies:
        copy.start()
    me, half = info[0], info[1]
    width = 2 * HD
    wide = 2 * rows_of
    lane = lax.broadcasted_iota(jnp.int32, (wide, width), 1)
    low_half = lane < HD
    first = lane % HD < HD // 2
    for r in range(2):
        total = None
        for k in range(planes):
            for side in range(2):
                chosen = half if side == 0 else 1 - half
                pair = (me ^ (PLANE * k + 2 * chosen)) // 2
                if r == 0:
                    copies[2 * k + side].wait()
                term = jnp.dot(
                    nb_ref[pair, r * wide:(r + 1) * wide, :], weights[2 * k + side],
                    preferred_element_type=jnp.float32,
                )
                total = term if total is None else total + term
        at = slice(r * wide, (r + 1) * wide)
        for g in range(kv_heads):
            tile = total[:, g * width:(g + 1) * width]
            tile = turn(tile, first, cos_ref[at, :], sin_ref[at, :]) * SCALE
            moved = pltpu.roll(tile, HD, 1)
            if g % 2 == 0:
                heads = (jnp.where(low_half, tile, 0.0), jnp.where(low_half, moved, 0.0))
            else:
                heads = (jnp.where(low_half, 0.0, moved), jnp.where(low_half, 0.0, tile))
            for u in range(2):
                for m in range(2):
                    start = (2 * (2 * r + m) + u) * rows_of
                    q_ref[g, start:start + rows_of, :] = heads[u][
                        m * rows_of:(m + 1) * rows_of
                    ].astype(jnp.bfloat16)


def make_queries(info, nb, cosine, sine, weights, planes, cols):
    rows = cosine.shape[0]
    kv_heads = planes * cols // (2 * HD)

    def body(*refs):
        query_kernel(planes, kv_heads, rows // PLANE, *refs)

    smem = pl.BlockSpec(memory_space=pltpu.SMEM)
    vmem = pl.BlockSpec(memory_space=pltpu.VMEM)
    anywhere = pl.BlockSpec(memory_space=pl.ANY)
    return pl.pallas_call(
        body,
        out_shape=jax.ShapeDtypeStruct((kv_heads, 2 * rows, 2 * HD), jnp.bfloat16),
        in_specs=[smem] + [vmem] * 3 + [anywhere] * len(weights),
        out_specs=vmem,
        scratch_shapes=[
            pltpu.VMEM((len(weights),) + weights[0].shape, jnp.bfloat16),
            pltpu.SemaphoreType.DMA((len(weights),)),
        ],
        compiler_params=pltpu.CompilerParams(vmem_limit_bytes=56 * 1024 * 1024),
        cost_estimate=pl.CostEstimate(
            flops=8_000_000_000, bytes_accessed=8_000_000, transcendentals=0
        ),
    )(info, nb, cosine, sine, *weights)


def attention_kernel(planes, kv_heads, rows_of, info, lo_first, sink_ref, q_ref, lo_ref, pos_ref,
                     own_kv, y_kv, c_kv, cy_kv, out_ref, bias_ref, score_ref, max_ref, acc_ref):
    me = info[0]
    plane = me // PLANE
    rows = PLANE * rows_of
    width = 2 * HD
    wide = 2 * rows_of
    cols = out_ref.shape[2]
    earliest = lo_first[0]
    for m in range(1, PLANE):
        earliest = jnp.minimum(earliest, lo_first[m])

    def for_needed(act):
        def step(k, carry):
            other = plane ^ k

            @pl.when((other <= plane) & (earliest < (other + 1) * rows))
            def _():
                act(k)

            return carry

        lax.fori_loop(0, planes, step, 0)

    def chunk(k, lanes):
        at = pl.ds(pl.multiple_of(k * rows_of, rows_of), rows_of)
        return jnp.concatenate(
            [own_kv[at, lanes], y_kv[at, lanes], c_kv[at, lanes], cy_kv[at, lanes]], axis=0
        )

    key_iota = lax.broadcasted_iota(jnp.int32, (1, rows_of), 1)

    def set_bias(k):
        key_pos = jnp.concatenate(
            [(me ^ (PLANE * k + m)) * rows_of + key_iota for m in ORDER], axis=1
        )
        allowed = (key_pos >= lo_ref[...]) & (key_pos <= pos_ref[...])
        bias_ref[k] = jnp.where(allowed, 0.0, NEGATIVE)

    for_needed(set_bias)

    lane_q = lax.broadcasted_iota(jnp.int32, (wide, width), 1) < HD
    lane_k = lax.broadcasted_iota(jnp.int32, (rows, width), 1) < HD
    row_q = lax.broadcasted_iota(jnp.int32, (wide, width), 0) < rows_of

    def two_heads(pair, carry):
        key_lanes = pl.ds(pl.multiple_of(pair * width, width), width)
        val_lanes = pl.ds(pl.multiple_of((kv_heads // 2 + pair) * width, width), width)
        sinks = [
            jnp.where(row_q, sink_ref[4 * pair + 2 * i], sink_ref[4 * pair + 2 * i + 1])
            for i in range(2)
        ]
        for i in range(2):
            for m in range(PLANE):
                max_ref[i, m * wide:(m + 1) * wide, :] = sinks[i]

        def scores(k):
            keys = chunk(k, key_lanes)
            for m in range(PLANE):
                at = slice(m * wide, (m + 1) * wide)
                bias = bias_ref[k, m * rows_of:(m + 1) * rows_of, :]
                for i in range(2):
                    score = lax.dot_general(
                        q_ref[2 * pair + i, at, :], keys, (((1,), (1,)), ((), ())),
                        preferred_element_type=jnp.float32,
                    )
                    score = (score.reshape(2, rows_of, rows) + bias[None]).reshape(wide, rows)
                    score_ref[i, k, at, :] = score
                    top = max_ref[i, at, :]
                    for start in range(0, rows, width):
                        top = jnp.maximum(top, score[:, start:start + width])
                    max_ref[i, at, :] = top

        for_needed(scores)

        for i in range(2):
            mine = lane_q if i == 0 else ~lane_q
            for m in range(PLANE):
                at = slice(m * wide, (m + 1) * wide)
                top = jnp.max(max_ref[i, at, :], axis=1, keepdims=True)
                top = jnp.broadcast_to(top, (wide, width))
                max_ref[i, at, :] = top
                acc_ref[i, at, :] = jnp.where(mine, 0.0, jnp.exp(sinks[i] - top))

        def gather(k):
            values = chunk(k, val_lanes)
            for i in range(2):
                mine_k = lane_k if i == 0 else ~lane_k
                vals = jnp.where(mine_k, values, jnp.bfloat16(1.0))
                for m in range(PLANE):
                    at = slice(m * wide, (m + 1) * wide)
                    top = max_ref[i, at, :]
                    probs = jnp.concatenate(
                        [
                            jnp.exp(score_ref[i, k, at, start:start + width] - top).astype(
                                jnp.bfloat16
                            )
                            for start in range(0, rows, width)
                        ],
                        axis=1,
                    )
                    acc_ref[i, at, :] += jnp.dot(probs, vals, preferred_element_type=jnp.float32)

        for_needed(gather)

        for i in range(2):
            g = 2 * pair + i
            for m in range(PLANE):
                acc = acc_ref[i, m * wide:(m + 1) * wide, :]
                done = acc / pltpu.roll(acc, HD, 1)
                one, two = done[:rows_of], done[rows_of:]
                low = lane_q[:rows_of]
                if i == 0:
                    both = jnp.where(low, one, pltpu.roll(two, HD, 1))
                else:
                    both = jnp.where(low, pltpu.roll(one, HD, 1), two)
                both = both.astype(jnp.bfloat16)
                for j in range(width // cols):
                    out_ref[g * (width // cols) + j, m * rows_of:(m + 1) * rows_of, :] = both[
                        :, j * cols:(j + 1) * cols
                    ]
        return carry

    lax.fori_loop(0, kv_heads // 2, two_heads, 0)


def attend(info, lo_first, sinks, queries, lo, pos, kv, planes, cols):
    rows = pos.shape[0]
    kv_heads = queries.shape[0]

    def body(*refs):
        attention_kernel(planes, kv_heads, rows // PLANE, *refs)

    return whole_call(
        body,
        jax.ShapeDtypeStruct((planes, rows, cols), jnp.bfloat16),
        (info, lo_first, sinks, queries, lo, pos, *kv),
        scalars=3,
        scratch=[
            pltpu.VMEM((planes, rows, rows), jnp.float32),
            pltpu.VMEM((2, planes, 2 * rows, rows), jnp.float32),
            pltpu.VMEM((2, 2 * rows, 2 * HD), jnp.float32),
            pltpu.VMEM((2, 2 * rows, 2 * HD), jnp.float32),
        ],
        limit=58,
        flops=16_000_000_000,
    )


def project(info, attended, own, mine, twin, places):
    planes, rows, cols = attended.shape
    width = own.shape[1]
    padded = lane_padded(width)
    wide = rows // 2

    def body(info_ref, att_ref, own_ref, *rest):
        send_ref, keep_ref, att, weight = rest[2 * len(places):]
        plane, half = info_ref[0] // PLANE, info_ref[1]
        short = cols // 2
        weight[:cols, :] = own_ref[...]
        for k in range(planes):
            att[:, k * cols:(k + 1) * cols] = att_ref[plane ^ k]
        for i, ks in enumerate(places):
            for side in range(2):
                chosen = half if side == 0 else 1 - half
                for j, k in enumerate(ks):
                    at = pl.multiple_of(k * cols + chosen * short, short)
                    weight[pl.ds(at, short), :] = rest[side * len(places) + i][
                        j * short:(j + 1) * short, :width
                    ]
        for start in range(0, width, 640):
            lanes = slice(start, min(width, start + 640))
            send_ref[:, lanes] = jnp.dot(
                att[wide:], weight[:, lanes], preferred_element_type=jnp.float32
            ).astype(jnp.bfloat16)
            keep_ref[:, lanes] = jnp.dot(
                att[:wide], weight[:, lanes], preferred_element_type=jnp.float32
            )
        send_ref[:, width:] = jnp.zeros((wide, padded - width), jnp.bfloat16)
        keep_ref[:, width:] = jnp.zeros((wide, padded - width), jnp.float32)

    return whole_call(
        body,
        [
            jax.ShapeDtypeStruct((wide, padded), jnp.bfloat16),
            jax.ShapeDtypeStruct((wide, padded), jnp.float32),
        ],
        (info, attended, own, *mine, *twin),
        scratch=[
            pltpu.VMEM((rows, planes * cols), jnp.bfloat16),
            pltpu.VMEM((planes * cols, width), jnp.bfloat16),
        ],
        flops=4_000_000_000,
    )


def add_core(keep, got):
    rows, width = keep.shape[0] // 2, keep.shape[1]

    def body(keep_ref, got_ref, send_ref, rest_ref):
        rest_ref[...] = keep_ref[:rows] + got_ref[:rows].astype(jnp.float32)
        send_ref[...] = (keep_ref[rows:] + got_ref[rows:].astype(jnp.float32)).astype(jnp.bfloat16)

    return whole_call(
        body,
        [
            jax.ShapeDtypeStruct((rows, width), jnp.bfloat16),
            jax.ShapeDtypeStruct((rows, width), jnp.float32),
        ],
        (keep, got),
        scalars=0,
    )


def mix(tokens, keep, got, gain):
    rows, padded = tokens.shape
    width = gain.shape[0]

    def body(tokens_ref, keep_ref, got_ref, gain_ref, mixed_ref, in_ref):
        mixed = (
            tokens_ref[...].astype(jnp.float32) + keep_ref[...] + got_ref[...].astype(jnp.float32)
        ).astype(jnp.bfloat16)
        mixed_ref[...] = mixed
        values = mixed.astype(jnp.float32)
        mean = jnp.sum(values * values, axis=1, keepdims=True) / width
        in_ref[...] = (values * lax.rsqrt(mean + EPS) * gain_ref[...]).astype(jnp.bfloat16)

    shape = jax.ShapeDtypeStruct((rows, padded), jnp.bfloat16)
    gain = jnp.pad(gain, (0, padded - width))[None]
    return whole_call(body, [shape, shape], (tokens, keep, got, gain), scalars=0)


def finish(width, mixed, total, *got):
    rows = mixed.shape[0]

    def body(mixed_ref, total_ref, *rest):
        out_ref = rest[-1]
        for start in range(0, width, 128):
            size = min(128, width - start)
            lanes = slice(start, start + size)
            value = mixed_ref[:, lanes].astype(jnp.float32) + total_ref[:, lanes]
            for ref in rest[:-1]:
                value += ref[:, lanes].astype(jnp.float32)
            if size < 128:
                value = jnp.concatenate([value, jnp.zeros((rows, 128 - size), jnp.float32)], axis=1)
            out_ref[lanes, :] = value.T[:size].astype(jnp.bfloat16)

    out = jax.ShapeDtypeStruct((width, rows), jnp.bfloat16)
    return whole_call(body, out, (mixed, total, *got), scalars=0).T


def by_columns(hidden, down):
    return lax.dot_general(hidden, down, (((1,), (1,)), ((), ())), preferred_element_type=jnp.float32)


def expert(x, row_weights, slabs):
    rows, padded = x.shape
    width, hidden = slabs[0].shape[1:]

    def body(x_ref, row_ref, gate_ref, up_ref, down_ref, out_ref, held, acc, sem):
        copies = [
            pltpu.make_async_copy(ref.at[side], held.at[3 * side + i], sem.at[3 * side + i])
            for side in range(2)
            for i, ref in enumerate((gate_ref, up_ref, down_ref))
        ]
        for copy in copies[:3]:
            copy.start()

        def wait(side, i):
            for s in range(2):
                @pl.when(side == s)
                def _():
                    copies[3 * s + i].wait()
                    if s == 0:
                        copies[3 + i].start()

        def one_slab(side, carry):
            inputs = x_ref[:, :width]
            wait(side, 0)
            gate_val = jnp.dot(inputs, held[3 * side], preferred_element_type=jnp.float32)
            wait(side, 1)
            up_val = jnp.dot(inputs, held[3 * side + 1], preferred_element_type=jnp.float32)
            rows_in = ((up_val + 1.0) * gate_val * jax.nn.sigmoid(ALPHA * gate_val)).astype(
                jnp.bfloat16
            )
            wait(side, 2)
            term = by_columns(rows_in, held[3 * side + 2])

            @pl.when(side == 0)
            def _():
                acc[...] = term

            @pl.when(side == 1)
            def _():
                out_ref[:, :width] = ((acc[...] + term) * row_ref[...]).astype(jnp.bfloat16)

            return carry

        lax.fori_loop(0, 2, one_slab, 0)
        out_ref[:, width:] = jnp.zeros((rows, padded - width), jnp.bfloat16)

    vmem = pl.BlockSpec(memory_space=pltpu.VMEM)
    return pl.pallas_call(
        body,
        out_shape=jax.ShapeDtypeStruct((rows, padded), jnp.bfloat16),
        in_specs=[vmem, vmem] + [pl.BlockSpec(memory_space=pl.ANY)] * 3,
        out_specs=vmem,
        scratch_shapes=[
            pltpu.VMEM((6, width, hidden), jnp.bfloat16),
            pltpu.VMEM((rows, width), jnp.float32),
            pltpu.SemaphoreType.DMA((6,)),
        ],
        compiler_params=pltpu.CompilerParams(vmem_limit_bytes=48 * 1024 * 1024),
        cost_estimate=pl.CostEstimate(
            flops=12 * rows * width * hidden,
            bytes_accessed=12 * width * hidden,
            transcendentals=2 * rows * hidden,
        ),
    )(x, row_weights, *slabs)


def per_device(
    tokens,
    lengths,
    attn_gain,
    w_query,
    w_key,
    w_value,
    sinks,
    w_out,
    moe_gain,
    routes,
    route_weights,
    w_gate,
    w_up,
    w_down,
):
    tok_rows, model_width = tokens.shape
    devices = lax.axis_size("ctx")
    planes = devices // PLANE
    me = lax.axis_index("ctx")
    in_plane = me % PLANE
    half = lax.axis_index("groups") % 2
    info = jnp.stack([me, half]).astype(jnp.int32)
    cols = w_query.shape[1] // devices
    q_rows = w_query.shape[0]

    cores = [[i, i + 1] for i in range(0, devices, 2)]
    slabs = [
        lax.all_gather(w, "ctx", axis=0, tiled=True, axis_index_groups=cores)
        for w in (w_gate, w_up, jnp.swapaxes(w_down, 1, 2))
    ]

    parts = split_query(info, w_query, planes)
    got = [swap_with(parts[m], "ctx", m) for m in (1, 2, 3)]

    span = jnp.arange(tok_rows, dtype=jnp.int32)
    positions = jnp.concatenate([(me ^ m) * tok_rows + span for m in ORDER])
    cosine, sine = angle_tables(positions)
    tokens, normed, kv = prepare(
        tokens, attn_gain, w_key, w_value, routes, route_weights, cosine[:tok_rows], sine[:tok_rows],
        parts[1],
    )
    kv_width, fact_width = w_key.shape[1] + w_value.shape[1], 4 * TOP

    w_mine, w_rest, late_normed = own_half(info, [parts[0], *got], normed, [])
    w_of = {0: w_mine}
    w_of.update(forwarded(w_of, planes, 1))
    kv_of = {0: kv}
    kv_of.update(forwarded(kv_of, planes, 1))
    y_normed = swap_with(late_normed, "ctx", 2)
    w_of, kv_of, y_normed = together(w_of, kv_of, y_normed)

    w_twin = {k: swap_with(w_of[k], "groups", 1) for k in w_of if k}
    w_of.update(forwarded(w_of, planes, 2))
    for hops in range(2, planes.bit_length()):
        kv_of.update(forwarded(kv_of, planes, hops))
    across = planes // 2
    wo_half = half_rows(info, w_out, y_normed)
    wo_of = {across: swap_with(wo_half, "ctx", PLANE * across)}
    w_of, w_twin, kv_of, y_normed, wo_half, wo_of = together(
        w_of, w_twin, kv_of, y_normed, wo_half, wo_of
    )

    for hops in range(3, planes.bit_length()):
        w_of.update(forwarded(w_of, planes, hops))
    two = joined(normed, y_normed)
    nb = cut_pairs(two, swap_with(two, "ctx", 1), devices // 2, 2 * q_rows)
    for k in w_of:
        if k and k not in w_twin:
            w_of[k] = gate(w_of[k], nb)
            w_twin[k] = swap_with(w_of[k], "groups", 1)
    own_kv = joined(*[kv_of[k] for k in range(planes)])
    y_kv = swap_with(own_kv, "ctx", 2)
    wo_twin = [swap_with(wo_of[across], "groups", 1)]
    wo_got, wo_ks, known = [wo_of[across]], [[across]], [0, across]
    bit = across // 2
    while bit:
        wo_got.append(swap_with(joined(wo_half, *wo_got), "ctx", PLANE * bit))
        wo_ks.append([k ^ bit for k in known])
        known += wo_ks[-1]
        bit //= 2
    w_twin, own_kv, y_kv, wo_got, wo_twin = together(w_twin, own_kv, y_kv, wo_got, wo_twin)

    c_kv = swap_with(own_kv, "ctx", 1)
    cy_kv = swap_with(y_kv, "ctx", 1)
    q_weights = [w_of[0], w_rest]
    for k in range(1, planes):
        q_weights += [w_of[k], w_twin[k]]
    wo_twin += [swap_with(rows, "groups", 1) for rows in wo_got[1:]]

    experts_num = devices // SPLITS
    capacity = tok_rows * TOP * 17 // (16 * experts_num)
    padded = -(-capacity // 8) * 8

    def facts_of(block):
        return block[:, kv_width:kv_width + fact_width].reshape(planes, tok_rows, fact_width).astype(
            jnp.float32
        )

    own_facts, far_facts = facts_of(own_kv), facts_of(y_kv)
    mine_expert = (me // SPLITS).astype(jnp.float32)
    other_expert = ((me // SPLITS) ^ 1).astype(jnp.float32)
    earlier = (span[:, None] < span[None, :]).astype(jnp.bfloat16)
    slot_ids = jnp.arange(padded, dtype=jnp.float32)

    def chosen_rows(known, expert_id):
        match = known[:, :, :TOP] == expert_id
        hit = jnp.any(match, axis=2)
        weight = sum(known[:, :, i * TOP:(i + 1) * TOP] for i in (1, 2, 3))
        weight = jnp.sum(jnp.where(match, weight, 0.0), axis=2)
        slot = jnp.dot(hit.astype(jnp.bfloat16), earlier, preferred_element_type=jnp.float32)
        pick = hit[:, None, :] & (slot[:, None, :] == slot_ids[None, :, None])
        row_weight = jnp.sum(jnp.where(pick, weight[:, None, :], 0.0), axis=2)
        return pick.astype(jnp.bfloat16), row_weight

    pick_own, weight_own = chosen_rows(own_facts, mine_expert)
    pick_other, _ = chosen_rows(own_facts, other_expert)
    _, weight_far = chosen_rows(far_facts, mine_expert)
    doc_ends = jnp.cumsum(lengths)
    lo = jnp.max(jnp.where(doc_ends[None, :] <= positions[:, None], doc_ends[None, :], 0), axis=1)
    heads_of = cols // HD
    my_sinks = lax.dynamic_index_in_dim(
        sinks.reshape(planes, PLANE, heads_of), in_plane, 1, keepdims=False
    ).reshape(-1)
    queries = make_queries(info, nb, cosine, sine, q_weights, planes, cols)
    attended = attend(
        info, lo[::tok_rows], my_sinks, queries, lo[:, None], positions[:, None],
        (own_kv, y_kv, c_kv, cy_kv), planes, cols,
    )
    send, keep = project(info, attended, w_out, wo_got, wo_twin, wo_ks)
    send, keep = add_core(keep, swap_with(send, "ctx", 1))
    mixed, expert_in = mix(tokens, keep, swap_with(send, "ctx", 2), moe_gain)

    def rows_for(pick, k, block):
        return jnp.dot(pick[k], block, preferred_element_type=jnp.float32).astype(jnp.bfloat16)

    def sent(k, block):
        rows = rows_for(pick_other, k, block)
        return rows, swap_with(rows, "ctx", 2)

    last = planes - 1
    near, far, ready = {}, {}, []
    first_rows, far[0] = sent(0, expert_in)
    blocks = over_planes(expert_in, planes)
    for k in range(planes - 1):
        near[k] = rows_for(pick_own, k, blocks[k])
        if k:
            rows, far[k] = sent(k, blocks[k])
            ready.append(rows)

    def run(parts):
        x = jnp.concatenate([rows for rows, _ in parts], axis=0)
        weights = jnp.concatenate([weight for _, weight in parts])
        out = expert(after(x, *ready), weights[:, None], slabs)
        return [out[i * padded:(i + 1) * padded] for i in range(len(parts))]

    done, back = {}, {}
    first = run([(near[k], weight_own[k]) for k in range(last)] + [(far[0], weight_far[0])])
    for k in range(last):
        done[k] = first[k]
    back[0] = swap_with(first[last], "ctx", 2)
    block = after(blocks[last], first[0])
    _, far[last] = sent(last, block)
    near[last] = rows_for(pick_own, last, block)
    middle = list(range(1, last))
    second = run(
        [(near[last], weight_own[last]), (far[last], weight_far[last])]
        + [(far[k], weight_far[k]) for k in middle]
    )
    done[last] = second[0]
    back[last] = swap_with(second[1], "ctx", 2)
    late = after(jnp.concatenate(second[2:], axis=0), back[last])
    late = swap_with(late, "ctx", 2)
    for i, k in enumerate(middle):
        back[k] = late[i * padded:(i + 1) * padded]

    def gathered(pick, k, rows):
        return lax.dot_general(
            pick[k], rows, (((0,), (0,)), ((), ())), preferred_element_type=jnp.float32
        )

    sums = {k: gathered(pick_own, k, done[k]) + gathered(pick_other, k, back[k]) for k in done}
    ends = []
    bit = 1
    while bit < planes:
        for k in sorted(sums, reverse=True):
            if k & bit:
                arrived = swap_with(sums.pop(k).astype(jnp.bfloat16), "ctx", PLANE * bit)
                if k ^ bit:
                    sums[k ^ bit] = sums[k ^ bit] + arrived.astype(jnp.float32)
                else:
                    ends.append(arrived)
        bit *= 2
    return finish(model_width, mixed, sums[0], *ends)


def solution(mesh):
    placed = (
        P(("groups", "ctx"), None),
        P("groups"),
        P(),
        P("ctx", None),
        P(),
        P(),
        P(),
        P("ctx", None),
        P(),
        P(("groups", "ctx"), None),
        P(("groups", "ctx"), None),
        P("ctx", None, None),
        P("ctx", None, None),
        P("ctx", None, None),
    )
    return jax.shard_map(
        per_device,
        mesh=mesh,
        in_specs=placed,
        out_specs=P(("groups", "ctx"), None),
        check_vma=False,
    )
```

```python
import jax
import jax.numpy as jnp
import numpy as np
from jax import lax
from jax.experimental import pallas as pl
from jax.experimental.pallas import tpu as pltpu
from jax.sharding import PartitionSpec as P

HD = 64
SPLITS = 2
TOP = 4
PLANE = 4
ORDER = (0, 2, 1, 3)

EPS = 1e-05
THETA = 150000.0
ALPHA = 1.702
SCALE = 0.125
NEGATIVE = -1e30


def swap_with(x, axis, bits):
    return lax.ppermute(x, axis, [(i, i ^ bits) for i in range(lax.axis_size(axis))])


def after(value, *earlier):
    return lax.optimization_barrier((value, *earlier))[0]


def gate(value, *earlier):
    anywhere = pl.BlockSpec(memory_space=pl.ANY)
    return pl.pallas_call(
        lambda *refs: None,
        out_shape=jax.ShapeDtypeStruct(value.shape, value.dtype),
        in_specs=[anywhere] * (1 + len(earlier)),
        out_specs=anywhere,
        input_output_aliases={0: 0},
    )(value, *earlier)


def forwarded(held, planes, hops):
    return {
        k: swap_with(held[k & (k - 1)], "ctx", PLANE * (k & -k))
        for k in range(planes - 1, 0, -1)
        if k.bit_count() == hops and k not in held
    }


def over_planes(block, planes):
    held = {0: block}
    for hops in range(1, planes.bit_length()):
        held.update(forwarded(held, planes, hops))
    return held


def together(*values):
    flat, tree = jax.tree.flatten(values)
    anywhere = pl.BlockSpec(memory_space=pl.ANY)
    out = pl.pallas_call(
        lambda *refs: None,
        out_shape=[jax.ShapeDtypeStruct(x.shape, x.dtype) for x in flat],
        in_specs=[anywhere] * len(flat),
        out_specs=[anywhere] * len(flat),
        input_output_aliases={i: i for i in range(len(flat))},
        compiler_params=pltpu.CompilerParams(vmem_limit_bytes=60 * 1024 * 1024),
    )(*flat)
    return jax.tree.unflatten(tree, out)


def lane_padded(width):
    return -(-width // 128) * 128


def rms_scale(values, gain_vec):
    wide = values.astype(jnp.float32)
    inverse = lax.rsqrt(jnp.mean(wide * wide, axis=-1, keepdims=True) + EPS)
    return (wide * inverse * gain_vec).astype(jnp.bfloat16)


def angle_tables(positions):
    half_size = HD // 2
    freqs = np.tile(THETA ** (-np.arange(half_size) / half_size), 4).astype(np.float32)
    sign = np.tile(np.repeat(np.array([-1.0, 1.0], np.float32), half_size), 2)
    angles = positions.astype(jnp.float32)[:, None] * freqs[None, :]
    return jnp.cos(angles), jnp.sin(angles) * sign[None, :]


def turn(tile, first, cosine, sine):
    width = 2 * HD
    other = jnp.where(first, pltpu.roll(tile, width - HD // 2, 1), pltpu.roll(tile, HD // 2, 1))
    return tile * cosine + other * sine


def whole_call(body, out_shapes, operands, scalars=1, scratch=(), limit=24, flops=0, waits=0):
    anywhere = pl.BlockSpec(memory_space=pl.ANY)
    smem = pl.BlockSpec(memory_space=pltpu.SMEM)
    vmem = pl.BlockSpec(memory_space=pltpu.VMEM)
    size = sum(x.size * x.dtype.itemsize for x in operands)
    return pl.pallas_call(
        body,
        out_shape=out_shapes,
        in_specs=[smem] * scalars + [vmem] * (len(operands) - scalars - waits) + [anywhere] * waits,
        out_specs=jax.tree.map(lambda _: vmem, out_shapes),
        scratch_shapes=list(scratch),
        compiler_params=pltpu.CompilerParams(vmem_limit_bytes=limit * 1024 * 1024),
        cost_estimate=pl.CostEstimate(flops=flops, bytes_accessed=size, transcendentals=0),
    )(*operands)


def split_query(info, w_query, planes):
    rows = w_query.shape[0]
    cols = w_query.shape[1] // (planes * PLANE)
    if cols % 128:
        in_plane = info[0] % PLANE
        parts = jnp.stack(
            [
                jnp.concatenate(
                    [
                        w_query[:, (PLANE * zz + j) * cols:(PLANE * zz + j + 1) * cols]
                        for zz in range(planes)
                    ],
                    axis=1,
                )
                for j in range(PLANE)
            ]
        )
        return [
            lax.dynamic_index_in_dim(parts, in_plane ^ m, 0, keepdims=False) for m in range(PLANE)
        ]

    def body(info_ref, w_ref, *outs):
        in_plane = info_ref[0] % PLANE
        for m in range(PLANE):
            for zz in range(planes):
                start = pl.multiple_of((PLANE * zz + (in_plane ^ m)) * cols, 128)
                outs[m][:, zz * cols:(zz + 1) * cols] = w_ref[:, pl.ds(start, cols)]

    shape = jax.ShapeDtypeStruct((rows, planes * cols), jnp.bfloat16)
    return whole_call(body, [shape] * PLANE, (info, w_query))


def prepare(tokens, gain, w_key, w_value, routes, route_weights, cosine, sine, earlier):
    rows, width = tokens.shape
    padded = lane_padded(width)
    key_cols = w_key.shape[1]

    def body(tok_ref, gain_ref, key_ref, val_ref, route_ref, weight_ref, cos_ref, sin_ref, _,
             rows_ref, normed_ref, kv_ref, wide):
        for start in range(0, width, 128):
            size = min(128, width - start)
            piece = tok_ref[start:start + size, :].astype(jnp.float32)
            if size < 128:
                piece = jnp.concatenate([piece, jnp.zeros((128 - size, rows), jnp.float32)], axis=0)
            wide[:, start:start + 128] = piece.T
        values = wide[...]
        rows_ref[...] = values.astype(jnp.bfloat16)
        mean = jnp.sum(values * values, axis=1, keepdims=True) / width
        normed_ref[...] = (values * lax.rsqrt(mean + EPS) * gain_ref[...]).astype(jnp.bfloat16)
        normed = normed_ref[:, :width]
        raw_key = jnp.dot(normed, key_ref[...], preferred_element_type=jnp.float32)
        lane = lax.broadcasted_iota(jnp.int32, (rows, 2 * HD), 1)
        first = lane % HD < HD // 2
        for start in range(0, key_cols, 2 * HD):
            lanes = slice(start, start + 2 * HD)
            kv_ref[:, lanes] = turn(raw_key[:, lanes], first, cos_ref[...], sin_ref[...]).astype(
                jnp.bfloat16
            )
        kv_ref[:, key_cols:2 * key_cols] = jnp.dot(
            normed, val_ref[...], preferred_element_type=jnp.float32
        ).astype(jnp.bfloat16)
        left = weight_ref[...]
        facts = [route_ref[...].astype(jnp.float32)]
        for _ in range(3):
            part = left.astype(jnp.bfloat16).astype(jnp.float32)
            facts.append(part)
            left = left - part
        facts.append(jnp.zeros((128 - 4 * TOP, rows), jnp.float32))
        kv_ref[:, 2 * key_cols:] = jnp.concatenate(facts, axis=0).T.astype(jnp.bfloat16)

    gain = jnp.pad(gain, (0, padded - width))[None]
    return whole_call(
        body,
        [
            jax.ShapeDtypeStruct((rows, padded), jnp.bfloat16),
            jax.ShapeDtypeStruct((rows, padded), jnp.bfloat16),
            jax.ShapeDtypeStruct((rows, 2 * key_cols + 128), jnp.bfloat16),
        ],
        (tokens.T, gain, w_key, w_value, routes.T, route_weights.T, cosine, sine, earlier),
        scalars=0,
        waits=1,
        scratch=[pltpu.VMEM((rows, padded), jnp.float32)],
        flops=1_000_000_000,
    )


def cut_pairs(two, c_two, pairs, cols):
    rows = two.shape[0]

    def body(two_ref, c_ref, out_ref):
        for b in range(pairs):
            lanes = slice(b * cols, (b + 1) * cols)
            out_ref[b, :rows, :] = two_ref[:, lanes]
            out_ref[b, rows:, :] = c_ref[:, lanes]

    return whole_call(
        body, jax.ShapeDtypeStruct((pairs, 2 * rows, cols), jnp.bfloat16), (two, c_two), scalars=0
    )


def joined(*blocks):
    rows = [block.shape[0] for block in blocks]

    def body(*refs):
        start = 0
        for ref, count in zip(refs[:-1], rows):
            refs[-1][start:start + count] = ref[...]
            start += count

    out = jax.ShapeDtypeStruct((sum(rows),) + blocks[0].shape[1:], blocks[0].dtype)
    return whole_call(body, out, blocks, scalars=0)


def half_rows(info, weight, earlier):
    rows, width = weight.shape
    padded = lane_padded(width)

    def body(info_ref, weight_ref, _, out_ref):
        at = pl.multiple_of(info_ref[1] * (rows // 2), rows // 2)
        out_ref[:, :width] = weight_ref[pl.ds(at, rows // 2), :]
        out_ref[:, width:] = jnp.zeros((rows // 2, padded - width), jnp.bfloat16)

    vmem = pl.BlockSpec(memory_space=pltpu.VMEM)
    return pl.pallas_call(
        body,
        out_shape=jax.ShapeDtypeStruct((rows // 2, padded), jnp.bfloat16),
        in_specs=[pl.BlockSpec(memory_space=pltpu.SMEM), vmem, pl.BlockSpec(memory_space=pl.ANY)],
        out_specs=vmem,
    )(info, weight, earlier)


def own_half(info, pieces, normed, earlier):
    rows, cols = pieces[0].shape

    def body(info_ref, p0, p1, p2, p3, normed_ref, *rest):
        mine_ref, rest_ref, again_ref = rest[-3:]
        odd = info_ref[0] % 2 == 1
        half = info_ref[1]
        again_ref[...] = normed_ref[...]
        for swapped in range(2):
            @pl.when(odd if swapped else jnp.logical_not(odd))
            def _():
                near = (p1, p0) if swapped else (p0, p1)
                far = (p3, p2) if swapped else (p2, p3)
                near = jnp.concatenate([near[0][...], near[1][...]], axis=0)
                far = jnp.concatenate([far[0][...], far[1][...]], axis=0)

                @pl.when(half == 0)
                def _():
                    mine_ref[...] = near
                    rest_ref[...] = far

                @pl.when(half == 1)
                def _():
                    mine_ref[...] = far
                    rest_ref[...] = near

    shape = jax.ShapeDtypeStruct((2 * rows, cols), jnp.bfloat16)
    again = jax.ShapeDtypeStruct(normed.shape, normed.dtype)
    return whole_call(
        body, [shape, shape, again], (info, *pieces, normed, *earlier), waits=len(earlier)
    )


def query_kernel(planes, kv_heads, rows_of, info, nb_ref, cos_ref, sin_ref, *rest):
    pieces = rest[: 2 * planes]
    q_ref, weights, sem = rest[2 * planes:]
    copies = [
        pltpu.make_async_copy(piece, weights.at[i], sem.at[i]) for i, piece in enumerate(pieces)
    ]
    for copy in copies:
        copy.start()
    me, half = info[0], info[1]
    width = 2 * HD
    wide = 2 * rows_of
    lane = lax.broadcasted_iota(jnp.int32, (wide, width), 1)
    low_half = lane < HD
    first = lane % HD < HD // 2
    for r in range(2):
        total = None
        for k in range(planes):
            for side in range(2):
                chosen = half if side == 0 else 1 - half
                pair = (me ^ (PLANE * k + 2 * chosen)) // 2
                if r == 0:
                    copies[2 * k + side].wait()
                term = jnp.dot(
                    nb_ref[pair, r * wide:(r + 1) * wide, :], weights[2 * k + side],
                    preferred_element_type=jnp.float32,
                )
                total = term if total is None else total + term
        at = slice(r * wide, (r + 1) * wide)
        for g in range(kv_heads):
            tile = total[:, g * width:(g + 1) * width]
            tile = turn(tile, first, cos_ref[at, :], sin_ref[at, :]) * SCALE
            moved = pltpu.roll(tile, HD, 1)
            if g % 2 == 0:
                heads = (jnp.where(low_half, tile, 0.0), jnp.where(low_half, moved, 0.0))
            else:
                heads = (jnp.where(low_half, 0.0, moved), jnp.where(low_half, 0.0, tile))
            for u in range(2):
                for m in range(2):
                    start = (2 * (2 * r + m) + u) * rows_of
                    q_ref[g, start:start + rows_of, :] = heads[u][
                        m * rows_of:(m + 1) * rows_of
                    ].astype(jnp.bfloat16)


def make_queries(info, nb, cosine, sine, weights, planes, cols):
    rows = cosine.shape[0]
    kv_heads = planes * cols // (2 * HD)

    def body(*refs):
        query_kernel(planes, kv_heads, rows // PLANE, *refs)

    smem = pl.BlockSpec(memory_space=pltpu.SMEM)
    vmem = pl.BlockSpec(memory_space=pltpu.VMEM)
    anywhere = pl.BlockSpec(memory_space=pl.ANY)
    return pl.pallas_call(
        body,
        out_shape=jax.ShapeDtypeStruct((kv_heads, 2 * rows, 2 * HD), jnp.bfloat16),
        in_specs=[smem] + [vmem] * 3 + [anywhere] * len(weights),
        out_specs=vmem,
        scratch_shapes=[
            pltpu.VMEM((len(weights),) + weights[0].shape, jnp.bfloat16),
            pltpu.SemaphoreType.DMA((len(weights),)),
        ],
        compiler_params=pltpu.CompilerParams(vmem_limit_bytes=56 * 1024 * 1024),
        cost_estimate=pl.CostEstimate(
            flops=8_000_000_000, bytes_accessed=8_000_000, transcendentals=0
        ),
    )(info, nb, cosine, sine, *weights)


def attention_kernel(planes, kv_heads, rows_of, info, lo_first, sink_ref, q_ref, lo_ref, pos_ref,
                     own_kv, y_kv, c_kv, cy_kv, out_ref, bias_ref, score_ref, max_ref, acc_ref):
    me = info[0]
    plane = me // PLANE
    rows = PLANE * rows_of
    width = 2 * HD
    wide = 2 * rows_of
    cols = out_ref.shape[2]
    earliest = lo_first[0]
    for m in range(1, PLANE):
        earliest = jnp.minimum(earliest, lo_first[m])

    def for_needed(act):
        def step(k, carry):
            other = plane ^ k

            @pl.when((other <= plane) & (earliest < (other + 1) * rows))
            def _():
                act(k)

            return carry

        lax.fori_loop(0, planes, step, 0)

    def chunk(k, lanes):
        at = pl.ds(pl.multiple_of(k * rows_of, rows_of), rows_of)
        return jnp.concatenate(
            [own_kv[at, lanes], y_kv[at, lanes], c_kv[at, lanes], cy_kv[at, lanes]], axis=0
        )

    key_iota = lax.broadcasted_iota(jnp.int32, (1, rows_of), 1)

    def set_bias(k):
        key_pos = jnp.concatenate(
            [(me ^ (PLANE * k + m)) * rows_of + key_iota for m in ORDER], axis=1
        )
        allowed = (key_pos >= lo_ref[...]) & (key_pos <= pos_ref[...])
        bias_ref[k] = jnp.where(allowed, 0.0, NEGATIVE)

    for_needed(set_bias)

    lane_q = lax.broadcasted_iota(jnp.int32, (wide, width), 1) < HD
    lane_k = lax.broadcasted_iota(jnp.int32, (rows, width), 1) < HD
    row_q = lax.broadcasted_iota(jnp.int32, (wide, width), 0) < rows_of

    def two_heads(pair, carry):
        key_lanes = pl.ds(pl.multiple_of(pair * width, width), width)
        val_lanes = pl.ds(pl.multiple_of((kv_heads // 2 + pair) * width, width), width)
        sinks = [
            jnp.where(row_q, sink_ref[4 * pair + 2 * i], sink_ref[4 * pair + 2 * i + 1])
            for i in range(2)
        ]
        for i in range(2):
            for m in range(PLANE):
                max_ref[i, m * wide:(m + 1) * wide, :] = sinks[i]

        def scores(k):
            keys = chunk(k, key_lanes)
            for m in range(PLANE):
                at = slice(m * wide, (m + 1) * wide)
                bias = bias_ref[k, m * rows_of:(m + 1) * rows_of, :]
                for i in range(2):
                    score = lax.dot_general(
                        q_ref[2 * pair + i, at, :], keys, (((1,), (1,)), ((), ())),
                        preferred_element_type=jnp.float32,
                    )
                    score = (score.reshape(2, rows_of, rows) + bias[None]).reshape(wide, rows)
                    score_ref[i, k, at, :] = score
                    top = max_ref[i, at, :]
                    for start in range(0, rows, width):
                        top = jnp.maximum(top, score[:, start:start + width])
                    max_ref[i, at, :] = top

        for_needed(scores)

        for i in range(2):
            mine = lane_q if i == 0 else ~lane_q
            for m in range(PLANE):
                at = slice(m * wide, (m + 1) * wide)
                top = jnp.max(max_ref[i, at, :], axis=1, keepdims=True)
                top = jnp.broadcast_to(top, (wide, width))
                max_ref[i, at, :] = top
                acc_ref[i, at, :] = jnp.where(mine, 0.0, jnp.exp(sinks[i] - top))

        def gather(k):
            values = chunk(k, val_lanes)
            for i in range(2):
                mine_k = lane_k if i == 0 else ~lane_k
                vals = jnp.where(mine_k, values, jnp.bfloat16(1.0))
                for m in range(PLANE):
                    at = slice(m * wide, (m + 1) * wide)
                    top = max_ref[i, at, :]
                    probs = jnp.concatenate(
                        [
                            jnp.exp(score_ref[i, k, at, start:start + width] - top).astype(
                                jnp.bfloat16
                            )
                            for start in range(0, rows, width)
                        ],
                        axis=1,
                    )
                    acc_ref[i, at, :] += jnp.dot(probs, vals, preferred_element_type=jnp.float32)

        for_needed(gather)

        for i in range(2):
            g = 2 * pair + i
            for m in range(PLANE):
                acc = acc_ref[i, m * wide:(m + 1) * wide, :]
                done = acc / pltpu.roll(acc, HD, 1)
                one, two = done[:rows_of], done[rows_of:]
                low = lane_q[:rows_of]
                if i == 0:
                    both = jnp.where(low, one, pltpu.roll(two, HD, 1))
                else:
                    both = jnp.where(low, pltpu.roll(one, HD, 1), two)
                both = both.astype(jnp.bfloat16)
                for j in range(width // cols):
                    out_ref[g * (width // cols) + j, m * rows_of:(m + 1) * rows_of, :] = both[
                        :, j * cols:(j + 1) * cols
                    ]
        return carry

    lax.fori_loop(0, kv_heads // 2, two_heads, 0)


def attend(info, lo_first, sinks, queries, lo, pos, kv, planes, cols):
    rows = pos.shape[0]
    kv_heads = queries.shape[0]

    def body(*refs):
        attention_kernel(planes, kv_heads, rows // PLANE, *refs)

    return whole_call(
        body,
        jax.ShapeDtypeStruct((planes, rows, cols), jnp.bfloat16),
        (info, lo_first, sinks, queries, lo, pos, *kv),
        scalars=3,
        scratch=[
            pltpu.VMEM((planes, rows, rows), jnp.float32),
            pltpu.VMEM((2, planes, 2 * rows, rows), jnp.float32),
            pltpu.VMEM((2, 2 * rows, 2 * HD), jnp.float32),
            pltpu.VMEM((2, 2 * rows, 2 * HD), jnp.float32),
        ],
        limit=58,
        flops=16_000_000_000,
    )


def project(info, attended, own, mine, twin, places):
    planes, rows, cols = attended.shape
    width = own.shape[1]
    padded = lane_padded(width)
    wide = rows // 2

    def body(info_ref, att_ref, own_ref, *rest):
        send_ref, keep_ref, att, weight = rest[2 * len(places):]
        plane, half = info_ref[0] // PLANE, info_ref[1]
        short = cols // 2
        weight[:cols, :] = own_ref[...]
        for k in range(planes):
            att[:, k * cols:(k + 1) * cols] = att_ref[plane ^ k]
        for i, ks in enumerate(places):
            for side in range(2):
                chosen = half if side == 0 else 1 - half
                for j, k in enumerate(ks):
                    at = pl.multiple_of(k * cols + chosen * short, short)
                    weight[pl.ds(at, short), :] = rest[side * len(places) + i][
                        j * short:(j + 1) * short, :width
                    ]
        for start in range(0, width, 640):
            lanes = slice(start, min(width, start + 640))
            send_ref[:, lanes] = jnp.dot(
                att[wide:], weight[:, lanes], preferred_element_type=jnp.float32
            ).astype(jnp.bfloat16)
            keep_ref[:, lanes] = jnp.dot(
                att[:wide], weight[:, lanes], preferred_element_type=jnp.float32
            )
        send_ref[:, width:] = jnp.zeros((wide, padded - width), jnp.bfloat16)
        keep_ref[:, width:] = jnp.zeros((wide, padded - width), jnp.float32)

    return whole_call(
        body,
        [
            jax.ShapeDtypeStruct((wide, padded), jnp.bfloat16),
            jax.ShapeDtypeStruct((wide, padded), jnp.float32),
        ],
        (info, attended, own, *mine, *twin),
        scratch=[
            pltpu.VMEM((rows, planes * cols), jnp.bfloat16),
            pltpu.VMEM((planes * cols, width), jnp.bfloat16),
        ],
        flops=4_000_000_000,
    )


def add_core(keep, got):
    rows, width = keep.shape[0] // 4, keep.shape[1]

    def body(keep_ref, got_ref, send_a, send_b, rest_a, rest_b):
        for i, (rest_ref, send_ref) in enumerate(((rest_a, send_a), (rest_b, send_b))):
            at = slice(i * rows, (i + 1) * rows)
            far = slice((2 + i) * rows, (3 + i) * rows)
            rest_ref[...] = keep_ref[at, :] + got_ref[at, :].astype(jnp.float32)
            send_ref[...] = (keep_ref[far, :] + got_ref[far, :].astype(jnp.float32)).astype(
                jnp.bfloat16
            )

    send = jax.ShapeDtypeStruct((rows, width), jnp.bfloat16)
    rest = jax.ShapeDtypeStruct((rows, width), jnp.float32)
    return whole_call(body, [send, send, rest, rest], (keep, got), scalars=0)


def mix(part, tokens, keep, got, gain):
    rows, padded = keep.shape
    width = gain.shape[0]

    def body(tokens_ref, keep_ref, got_ref, gain_ref, mixed_ref, in_ref):
        mixed = (
            tokens_ref[part * rows:(part + 1) * rows, :].astype(jnp.float32)
            + keep_ref[...]
            + got_ref[...].astype(jnp.float32)
        ).astype(jnp.bfloat16)
        mixed_ref[...] = mixed
        values = mixed.astype(jnp.float32)
        mean = jnp.sum(values * values, axis=1, keepdims=True) / width
        in_ref[...] = (values * lax.rsqrt(mean + EPS) * gain_ref[...]).astype(jnp.bfloat16)

    shape = jax.ShapeDtypeStruct((rows, padded), jnp.bfloat16)
    gain = jnp.pad(gain, (0, padded - width))[None]
    return whole_call(body, [shape, shape], (tokens, keep, got, gain), scalars=0)


def finish(width, parts):
    rows = sum(part[0].shape[0] for part in parts)
    operands = [x for part in parts for x in part]

    def body(*refs):
        out_ref = refs[-1]
        for start in range(0, width, 128):
            size = min(128, width - start)
            values, first = [], 0
            for part in parts:
                value = None
                for ref in refs[first:first + len(part)]:
                    term = ref[:, start:start + 128].astype(jnp.float32)
                    value = term if value is None else value + term
                values.append(value)
                first += len(part)
            value = jnp.concatenate(values, axis=0)
            out_ref[start:start + size, :] = value.T[:size].astype(jnp.bfloat16)

    out = jax.ShapeDtypeStruct((width, rows), jnp.bfloat16)
    return whole_call(body, out, operands, scalars=0).T


def by_columns(hidden, down):
    return lax.dot_general(hidden, down, (((1,), (1,)), ((), ())), preferred_element_type=jnp.float32)


def expert(x, row_weights, slabs):
    rows, padded = x.shape
    width, hidden = slabs[0].shape[1:]

    def body(x_ref, row_ref, gate_ref, up_ref, down_ref, out_ref, held, acc, sem):
        copies = [
            pltpu.make_async_copy(ref.at[side], held.at[3 * side + i], sem.at[3 * side + i])
            for side in range(2)
            for i, ref in enumerate((gate_ref, up_ref, down_ref))
        ]
        for copy in copies[:3]:
            copy.start()

        def wait(side, i):
            for s in range(2):
                @pl.when(side == s)
                def _():
                    copies[3 * s + i].wait()
                    if s == 0:
                        copies[3 + i].start()

        def one_slab(side, carry):
            inputs = x_ref[:, :width]
            wait(side, 0)
            gate_val = jnp.dot(inputs, held[3 * side], preferred_element_type=jnp.float32)
            wait(side, 1)
            up_val = jnp.dot(inputs, held[3 * side + 1], preferred_element_type=jnp.float32)
            rows_in = ((up_val + 1.0) * gate_val * jax.nn.sigmoid(ALPHA * gate_val)).astype(
                jnp.bfloat16
            )
            wait(side, 2)
            term = by_columns(rows_in, held[3 * side + 2])

            @pl.when(side == 0)
            def _():
                acc[...] = term

            @pl.when(side == 1)
            def _():
                out_ref[:, :width] = ((acc[...] + term) * row_ref[...]).astype(jnp.bfloat16)

            return carry

        lax.fori_loop(0, 2, one_slab, 0)
        out_ref[:, width:] = jnp.zeros((rows, padded - width), jnp.bfloat16)

    vmem = pl.BlockSpec(memory_space=pltpu.VMEM)
    return pl.pallas_call(
        body,
        out_shape=jax.ShapeDtypeStruct((rows, padded), jnp.bfloat16),
        in_specs=[vmem, vmem] + [pl.BlockSpec(memory_space=pl.ANY)] * 3,
        out_specs=vmem,
        scratch_shapes=[
            pltpu.VMEM((6, width, hidden), jnp.bfloat16),
            pltpu.VMEM((rows, width), jnp.float32),
            pltpu.SemaphoreType.DMA((6,)),
        ],
        compiler_params=pltpu.CompilerParams(vmem_limit_bytes=48 * 1024 * 1024),
        cost_estimate=pl.CostEstimate(
            flops=12 * rows * width * hidden,
            bytes_accessed=12 * width * hidden,
            transcendentals=2 * rows * hidden,
        ),
    )(x, row_weights, *slabs)


def per_device(
    tokens,
    lengths,
    attn_gain,
    w_query,
    w_key,
    w_value,
    sinks,
    w_out,
    moe_gain,
    routes,
    route_weights,
    w_gate,
    w_up,
    w_down,
):
    tok_rows, model_width = tokens.shape
    devices = lax.axis_size("ctx")
    planes = devices // PLANE
    me = lax.axis_index("ctx")
    in_plane = me % PLANE
    half = lax.axis_index("groups") % 2
    info = jnp.stack([me, half]).astype(jnp.int32)
    cols = w_query.shape[1] // devices
    q_rows = w_query.shape[0]

    cores = [[i, i + 1] for i in range(0, devices, 2)]
    slabs = [
        lax.all_gather(w, "ctx", axis=0, tiled=True, axis_index_groups=cores)
        for w in (w_gate, w_up, jnp.swapaxes(w_down, 1, 2))
    ]

    parts = split_query(info, w_query, planes)
    got = [swap_with(parts[m], "ctx", m) for m in (1, 2, 3)]

    span = jnp.arange(tok_rows, dtype=jnp.int32)
    positions = jnp.concatenate([(me ^ m) * tok_rows + span for m in ORDER])
    cosine, sine = angle_tables(positions)
    tokens, normed, kv = prepare(
        tokens, attn_gain, w_key, w_value, routes, route_weights, cosine[:tok_rows], sine[:tok_rows],
        parts[1],
    )
    kv_width, fact_width = w_key.shape[1] + w_value.shape[1], 4 * TOP

    w_mine, w_rest, late_normed = own_half(info, [parts[0], *got], normed, [])
    w_of = {0: w_mine}
    w_of.update(forwarded(w_of, planes, 1))
    kv_of = {0: kv}
    kv_of.update(forwarded(kv_of, planes, 1))
    y_normed = swap_with(late_normed, "ctx", 2)
    w_of, kv_of, y_normed = together(w_of, kv_of, y_normed)

    w_twin = {k: swap_with(w_of[k], "groups", 1) for k in w_of if k}
    w_of.update(forwarded(w_of, planes, 2))
    for hops in range(2, planes.bit_length()):
        kv_of.update(forwarded(kv_of, planes, hops))
    across = planes // 2
    wo_half = half_rows(info, w_out, y_normed)
    wo_of = {across: swap_with(wo_half, "ctx", PLANE * across)}
    w_of, w_twin, kv_of, y_normed, wo_half, wo_of = together(
        w_of, w_twin, kv_of, y_normed, wo_half, wo_of
    )

    for hops in range(3, planes.bit_length()):
        w_of.update(forwarded(w_of, planes, hops))
    two = joined(normed, y_normed)
    nb = cut_pairs(two, swap_with(two, "ctx", 1), devices // 2, 2 * q_rows)
    for k in w_of:
        if k and k not in w_twin:
            w_of[k] = gate(w_of[k], nb)
            w_twin[k] = swap_with(w_of[k], "groups", 1)
    own_kv = joined(*[kv_of[k] for k in range(planes)])
    y_kv = swap_with(own_kv, "ctx", 2)
    wo_twin = [swap_with(wo_of[across], "groups", 1)]
    wo_got, wo_ks, known = [wo_of[across]], [[across]], [0, across]
    bit = across // 2
    while bit:
        wo_got.append(swap_with(joined(wo_half, *wo_got), "ctx", PLANE * bit))
        wo_ks.append([k ^ bit for k in known])
        known += wo_ks[-1]
        bit //= 2
    w_twin, own_kv, y_kv, wo_got, wo_twin = together(w_twin, own_kv, y_kv, wo_got, wo_twin)

    c_kv = swap_with(own_kv, "ctx", 1)
    cy_kv = swap_with(y_kv, "ctx", 1)
    q_weights = [w_of[0], w_rest]
    for k in range(1, planes):
        q_weights += [w_of[k], w_twin[k]]
    wo_twin += [swap_with(rows, "groups", 1) for rows in wo_got[1:]]

    experts_num = devices // SPLITS
    capacity = tok_rows * TOP * 17 // (16 * experts_num)
    padded = -(-capacity // 8) * 8

    def facts_of(block):
        return block[:, kv_width:kv_width + fact_width].reshape(planes, tok_rows, fact_width).astype(
            jnp.float32
        )

    own_facts, far_facts = facts_of(own_kv), facts_of(y_kv)
    mine_expert = (me // SPLITS).astype(jnp.float32)
    other_expert = ((me // SPLITS) ^ 1).astype(jnp.float32)
    earlier = (span[:, None] < span[None, :]).astype(jnp.bfloat16)
    slot_ids = jnp.arange(padded, dtype=jnp.float32)

    def chosen_rows(known, expert_id):
        match = known[:, :, :TOP] == expert_id
        hit = jnp.any(match, axis=2)
        weight = sum(known[:, :, i * TOP:(i + 1) * TOP] for i in (1, 2, 3))
        weight = jnp.sum(jnp.where(match, weight, 0.0), axis=2)
        slot = jnp.dot(hit.astype(jnp.bfloat16), earlier, preferred_element_type=jnp.float32)
        pick = hit[:, None, :] & (slot[:, None, :] == slot_ids[None, :, None])
        row_weight = jnp.sum(jnp.where(pick, weight[:, None, :], 0.0), axis=2)
        return pick.astype(jnp.bfloat16), row_weight

    pick_own, weight_own = chosen_rows(own_facts, mine_expert)
    pick_other, _ = chosen_rows(own_facts, other_expert)
    _, weight_far = chosen_rows(far_facts, mine_expert)
    doc_ends = jnp.cumsum(lengths)
    lo = jnp.max(jnp.where(doc_ends[None, :] <= positions[:, None], doc_ends[None, :], 0), axis=1)
    heads_of = cols // HD
    my_sinks = lax.dynamic_index_in_dim(
        sinks.reshape(planes, PLANE, heads_of), in_plane, 1, keepdims=False
    ).reshape(-1)
    queries = make_queries(info, nb, cosine, sine, q_weights, planes, cols)
    attended = attend(
        info, lo[::tok_rows], my_sinks, queries, lo[:, None], positions[:, None],
        (own_kv, y_kv, c_kv, cy_kv), planes, cols,
    )
    send, keep = project(info, attended, w_out, wo_got, wo_twin, wo_ks)
    *sends, keep_a, keep_b = add_core(keep, swap_with(send, "ctx", 1))
    got_a = swap_with(sends[0], "ctx", 2)
    mixed_a, in_a = mix(0, tokens, keep_a, got_a, moe_gain)
    blocks_a = over_planes(in_a, planes)
    got_b = swap_with(gate(sends[1], got_a), "ctx", 2)
    mixed_b, in_b = mix(1, tokens, keep_b, got_b, moe_gain)
    blocks_b = over_planes(in_b, planes)

    def rows_for(pick, k, block):
        return jnp.dot(pick[k], block, preferred_element_type=jnp.float32).astype(jnp.bfloat16)

    def sent(k, block):
        rows = rows_for(pick_other, k, block)
        return rows, swap_with(rows, "ctx", 2)

    last = planes - 1
    near, far, ready = {}, {}, []
    blocks = {k: joined(blocks_a[k], blocks_b[k]) for k in range(planes)}
    first_rows, far[0] = sent(0, blocks[0])
    for k in range(planes - 1):
        near[k] = rows_for(pick_own, k, blocks[k])
        if k:
            rows, far[k] = sent(k, blocks[k])
            ready.append(rows)

    def run(parts):
        x = jnp.concatenate([rows for rows, _ in parts], axis=0)
        weights = jnp.concatenate([weight for _, weight in parts])
        out = expert(after(x, *ready), weights[:, None], slabs)
        return [out[i * padded:(i + 1) * padded] for i in range(len(parts))]

    done, back = {}, {}
    first = run([(near[k], weight_own[k]) for k in range(last)] + [(far[0], weight_far[0])])
    for k in range(last):
        done[k] = first[k]
    back[0] = swap_with(first[last], "ctx", 2)
    block = after(blocks[last], first[0])
    _, far[last] = sent(last, block)
    near[last] = rows_for(pick_own, last, block)
    middle = list(range(1, last))
    second = run(
        [(near[last], weight_own[last]), (far[last], weight_far[last])]
        + [(far[k], weight_far[k]) for k in middle]
    )
    done[last] = second[0]
    back[last] = swap_with(second[1], "ctx", 2)
    late = after(jnp.concatenate(second[2:], axis=0), back[last])
    late = swap_with(late, "ctx", 2)
    for i, k in enumerate(middle):
        back[k] = late[i * padded:(i + 1) * padded]

    def gathered(pick, k, rows):
        return lax.dot_general(
            pick[k], rows, (((0,), (0,)), ((), ())), preferred_element_type=jnp.float32
        )

    sums = {k: gathered(pick_own, k, done[k]) + gathered(pick_other, k, back[k]) for k in done}
    ends = []
    bit = 1
    while bit < planes:
        for k in sorted(sums, reverse=True):
            if k & bit:
                arrived = swap_with(sums.pop(k).astype(jnp.bfloat16), "ctx", PLANE * bit)
                if k ^ bit:
                    sums[k ^ bit] = sums[k ^ bit] + arrived.astype(jnp.float32)
                else:
                    ends.append(arrived)
        bit *= 2
    return finish(model_width, [[joined(mixed_a, mixed_b), sums[0], *ends]])


def solution(mesh):
    placed = (
        P(("groups", "ctx"), None),
        P("groups"),
        P(),
        P("ctx", None),
        P(),
        P(),
        P(),
        P("ctx", None),
        P(),
        P(("groups", "ctx"), None),
        P(("groups", "ctx"), None),
        P("ctx", None, None),
        P("ctx", None, None),
        P("ctx", None, None),
    )
    return jax.shard_map(
        per_device,
        mesh=mesh,
        in_specs=placed,
        out_specs=P(("groups", "ctx"), None),
        check_vma=False,
    )
```
